512 devices in a mesh: member: 16 (over y_lo, x, core), space: 32 (over z, y_hi).
Axes of the slice: x: 4, y: 4 (y_hi: 2, y_lo: 2; y = y_hi * 2 + y_lo), z: 16, core: 2. Of those that a mesh axis runs over, the one named last changes fastest.
Arguments:
- depth: float32 [32, 512, 2048], P('member', 'space'), may hold values from 0.05 to 3
- flow_x: float32 [32, 512, 2048], P('member', 'space'), may hold values from -3 to 3
- flow_y: float32 [32, 512, 2048], P('member', 'space'), may hold values from -3 to 3
- terrain: float32 [512, 2048], P('space'), may hold values from -3 to 3
- roughness: float32 [512, 2048], P('space'), may hold values from 0.02 to 0.12
- gauges: int32 [512], replicated, may hold values from 0 to 1048575
- observed: float32 [512], replicated, may hold values from 4 to 6
- ancestors: int32 [32], replicated, may hold values from 0 to 31, as said below
Outputs:
- depth_out: float32 [32, 512, 2048], P('member', 'space')
- flow_x_out: float32 [32, 512, 2048], P('member', 'space')
- flow_y_out: float32 [32, 512, 2048], P('member', 'space')
- log_weight: float32 [32], P('member')
The draws below stay inside these ranges and needn't reach their ends.
Inputs may be any that keep to these rules, and one draw needn't show every extreme that they name: `ancestors`: each entry names a particle.
All inputs are finite; a program needn't handle non-finite values.
Results may differ from the reference program's by a relative error of at most 0.0003.
Values sent between devices are 32-bit elements; how exact they have to be, the bound alone decides.
A program may use at most 128 MiB of HBM per device.

```python
import math
import jax
import jax.numpy as jnp
from jax import lax

P_DEV = 2
W = 2048
STEPS = 2
GAUGES = 512
PARTICLES = 32
NX = 512


def draw_ancestors(key, part):
    key = jax.random.fold_in(key, 7)
    key_perm = jax.random.fold_in(key, 1)
    key_first = jax.random.fold_in(key, 2)
    key_second = jax.random.fold_in(key, 3)
    key_slot = jax.random.fold_in(key, 4)
    order = jax.random.permutation(key_perm, PARTICLES).astype(jnp.int32)
    first_pick = jax.random.randint(key_first, (PARTICLES,), 0, PARTICLES, dtype=jnp.int32)
    second_pick = jax.random.randint(key_second, (PARTICLES,), 0, PARTICLES, dtype=jnp.int32)
    skewed = order[jnp.minimum(first_pick, second_pick)]
    members = PARTICLES // P_DEV
    new_index = jnp.arange(PARTICLES, dtype=jnp.int32)
    owner = new_index // P_DEV
    before = (owner + members - 1) % members
    slot_pick = jax.random.randint(key_slot, (PARTICLES,), 0, P_DEV, dtype=jnp.int32)
    from_before = before * P_DEV + slot_pick
    return jnp.where(new_index % P_DEV == 0, from_before, skewed).astype(jnp.int32)


def plant(result, rng, smallest, top_value):
    shape = result.shape
    spot = [jax.random.randint(jax.random.fold_in(rng, axis), (), 0, shape[axis]) for axis in range(len(shape))]
    result = result.at[tuple(spot)].set(smallest)
    longest = shape.index(max(shape))
    spot[longest] = (spot[longest] + 1) % shape[longest]
    return result.at[tuple(spot)].set(top_value)


def block_levels(stream_key, dims, pieces, least, top_value):
    gain = 1.0
    for dim, parts in pieces:
        heights = jax.random.uniform(jax.random.fold_in(jax.random.fold_in(stream_key, 6), dim), (parts,), jnp.float32, least / len(pieces), top_value / len(pieces))
        gain = gain * jnp.repeat(jnp.exp(heights), dims[dim] // parts).reshape((-1,) + (1,) * (len(dims) - 1 - dim))
    return gain


def normal_values(stream_key, extent, spread, bound, split=(), held_as=jnp.bfloat16):
    factor_of = block_levels(stream_key, extent, split, -0.22, 0.18) if split else 1.0
    result = jax.random.normal(stream_key, extent, jnp.float32) * spread * factor_of
    return jnp.minimum(jnp.maximum(result, -bound), bound).astype(held_as)


def setup_inputs(seed: int = 0) -> dict:
    seeds = jax.random.split(jax.random.key(seed), 9)
    return {
        "depth": jnp.clip(jnp.exp(math.log(3.0) - 4.0943445 * jax.random.uniform(seeds[0], (PARTICLES, NX, W), jnp.float32) ** block_levels(seeds[0], (PARTICLES, NX, W), ((0, 16), (1, 32)), -0.2, 0.2)), 0.05, 3.0),
        "flow_x": normal_values(seeds[1], (PARTICLES, NX, W), 0.3, 3.0, ((0, 16), (1, 32)), jnp.float32),
        "flow_y": normal_values(seeds[2], (PARTICLES, NX, W), 0.3, 3.0, ((0, 16), (1, 32)), jnp.float32),
        "terrain": normal_values(seeds[3], (NX, W), 0.5, 3.0, ((0, 32),), jnp.float32),
        "roughness": jnp.clip(jnp.exp(math.log(0.12) - 1.7917595 * jax.random.uniform(seeds[4], (NX, W), jnp.float32) ** block_levels(seeds[4], (NX, W), ((0, 32),), -0.2, 0.2)), 0.02, 0.12),
        "gauges": plant(jax.random.randint(seeds[5], (GAUGES,), 0, NX * W), jax.random.fold_in(seeds[5], 1), 0, (NX * W) - 1).astype(jnp.int32),
        "observed": jnp.clip(jax.random.uniform(seeds[6], (GAUGES,), jnp.float32, 4.0, 6.0), 4.0, 6.0),
        "ancestors": draw_ancestors(jax.random.fold_in(seeds[8], 71), 0),
    }


gravity = 9.81
time_step = 1.0
cell_size = 30.0
depth_floor = 0.1


def face_flux(flow, eta_a, eta_b, bed_a, bed_b, rough):
    hflow = jnp.maximum(jnp.maximum(eta_a, eta_b) - jnp.maximum(bed_a, bed_b), depth_floor)
    slope = (eta_b - eta_a) / cell_size
    return (flow - gravity * hflow * time_step * slope) / (1.0 + gravity * time_step * rough * rough * jnp.abs(flow) / jnp.power(hflow, 7.0 / 3.0))


def advance(depth, flow_x, flow_y, terrain, roughness):
    eta = terrain + depth
    east = face_flux(flow_x[:, :-1], eta[:, :-1], eta[:, 1:], terrain[:, :-1], terrain[:, 1:], roughness[:, :-1])
    east = jnp.concatenate([east, jnp.zeros((depth.shape[0], 1), jnp.float32)], axis=1)
    south = face_flux(flow_y[:-1], eta[:-1], eta[1:], terrain[:-1], terrain[1:], roughness[:-1])
    south = jnp.concatenate([south, jnp.zeros((1, depth.shape[1]), jnp.float32)], axis=0)
    west = jnp.concatenate([jnp.zeros((depth.shape[0], 1), jnp.float32), east[:, :-1]], axis=1)
    north = jnp.concatenate([jnp.zeros((1, depth.shape[1]), jnp.float32), south[:-1]], axis=0)
    return depth + (time_step / cell_size) * (west - east + north - south), east, south


def reference(depth, flow_x, flow_y, terrain, roughness, gauges, observed, ancestors):
    def forward(state):
        water, east, south = state
        for step in range(STEPS):
            water, east, south = advance(water, east, south, terrain, roughness)
        return water, east, south

    def first(state):
        water, east, south = forward(state)
        values = jnp.take(water.reshape(-1), gauges)
        loglik = -0.5 * jnp.sum((values - observed) ** 2)
        return water, east, south, loglik

    water, east, south, loglik = lax.map(first, (depth, flow_x, flow_y))
    top = jnp.max(loglik)
    log_weight = loglik - top - jnp.log(jnp.sum(jnp.exp(loglik - top)))
    water = jnp.take(water, ancestors, axis=0)
    east = jnp.take(east, ancestors, axis=0)
    south = jnp.take(south, ancestors, axis=0)
    water, east, south = lax.map(forward, (water, east, south))
    return water, east, south, log_weight
```

```python
import functools

import jax
import jax.numpy as jnp
from jax import lax
from jax.experimental import pallas as pl
from jax.experimental.pallas import tpu as pltpu
from jax.sharding import PartitionSpec as P

MESH = pl.DeviceIdType.MESH
gravity = 9.81
time_step = 1.0
cell_size = 30.0
depth_floor = 0.1

EAST, WATER, SOUTH = 0, 1, 2
ROWS = 16
LANES = 128
PARTS = 2
SUB = 16
RIM = 2
EXT = ROWS + 2 * RIM
BARS = (4, 4, 2)
HOLDERS = 9
VMEM_LIMIT = 48 * 2**20


def next_column(x):
    y = pltpu.roll(x, LANES - 1, 1)
    lane = lax.broadcasted_iota(jnp.int32, x.shape, 1)
    return jnp.where(lane == LANES - 1, pltpu.roll(y, SUB - 1, 0), y)


def previous_column(x):
    y = pltpu.roll(x, 1, 1)
    lane = lax.broadcasted_iota(jnp.int32, x.shape, 1)
    return jnp.where(lane == 0, pltpu.roll(y, 1, 0), y)


def face(flow, eta_a, eta_b, bed_top, friction):
    hflow = jnp.maximum(jnp.maximum(eta_a, eta_b) - bed_top, depth_floor)
    push = flow - (gravity * time_step / cell_size) * hflow * (eta_b - eta_a)
    drag = 1.0 + friction * jnp.abs(flow) * jnp.exp(jnp.log(hflow) * (-7.0 / 3.0))
    inverse = pl.reciprocal(drag, approx=True)
    inverse = inverse * (2.0 - drag * inverse)
    return push * inverse


def south_flow(src, bed, row, first, last_row):
    at = row + RIM
    bed_a, bed_b = bed[at, 0], bed[at + 1, 0]
    bed_top = jnp.maximum(bed_a, bed_b)
    friction = bed[at, 1]
    ok = jnp.logical_and(first + row >= 0, first + row < last_row)
    out = []
    for p in range(PARTS):
        eta_a = bed_a + src[3 * at + WATER, p]
        eta_b = bed_b + src[3 * (at + 1) + WATER, p]
        flow = face(src[3 * at + SOUTH, p], eta_a, eta_b, bed_top, friction)
        out.append(jnp.where(ok, flow, 0.0))
    return tuple(out)


def step_rows(src, bed, low, count, first, last_row, store):
    sub = lax.broadcasted_iota(jnp.int32, (SUB, LANES), 0)
    lane = lax.broadcasted_iota(jnp.int32, (SUB, LANES), 1)
    rim = jnp.logical_and(sub == SUB - 1, lane == LANES - 1)

    def one(i, north):
        row = low + i
        at = row + RIM
        south = south_flow(src, bed, row, first, last_row)
        bed_a = bed[at, 0]
        bed_top = jnp.maximum(bed_a, next_column(bed_a))
        friction = bed[at, 1]
        for p in range(PARTS):
            water = src[3 * at + WATER, p]
            eta = bed_a + water
            east = face(src[3 * at + EAST, p], eta, next_column(eta), bed_top, friction)
            east = jnp.where(rim, 0.0, east)
            west = previous_column(east)
            new = water + (time_step / cell_size) * (west - east + north[p] - south[p])
            store(row, p, EAST, east)
            store(row, p, WATER, new)
            store(row, p, SOUTH, south[p])
        return south

    lax.fori_loop(0, count, one, south_flow(src, bed, low - 1, first, last_row))


def keep_in(dst, rim):
    def store(row, p, field, value):
        dst[3 * (row + rim) + field, p] = value

    return store


def exchange_kernel(
    members, slabs,
    water_in, east_in, south_in, bed_in, rough_in, gauges, observed, ancestors,
    state_out, bed_out, lik_out,
    raw, raw_bed, a, b, c, bed, held, held_rim, out, out_rim, sums, got,
    in_sem, halo_send, halo_recv, s1, r1, sh, rh, s2, r2, s2h, r2h, ls, lr, ms, mr, own_sem,
):
    m = lax.axis_index("member")
    s = lax.axis_index("space")
    up = lax.rem(s + slabs - 1, slabs)
    down = lax.rem(s + 1, slabs)
    across = lax.rem(m + members // 2, members)
    first = s * ROWS
    last_row = slabs * ROWS - 1
    rim_at = m // 2 + 8 * lax.rem(m, 2)
    rim_slot = 1 + rim_at + 48 * (rim_at // 5) + rim_at // 8

    def remote(src, dst, send, recv, member, slab):
        return pltpu.make_async_remote_copy(
            src_ref=src, dst_ref=dst, send_sem=send, recv_sem=recv,
            device_id=(member, slab), device_id_type=MESH,
        )

    loads = [
        pltpu.make_async_copy(ref, raw.at[i], in_sem.at[i])
        for i, ref in enumerate((east_in, water_in, south_in))
    ] + [
        pltpu.make_async_copy(ref, raw_bed.at[i], in_sem.at[3 + i])
        for i, ref in enumerate((bed_in, rough_in))
    ]
    for copy in loads:
        copy.start()

    ring = []
    stride = 1
    for size in BARS:
        digit = lax.rem(s // stride, size)
        ring.append([
            s + (lax.rem(digit + i, size) - digit) * stride for i in range(1, size)
        ])
        stride *= size
    holder = [(2 * i if i < 8 else 1, down if i < 5 else up) for i in range(HOLDERS)]

    barrier = pltpu.get_barrier_semaphore()

    def greet(member, slab):
        pl.semaphore_signal(barrier, inc=1, device_id=(member, slab), device_id_type=MESH)

    for slab in (up, down):
        greet(m, slab)
        greet(across, slab)

    @pl.loop(1, members)
    def _(i):
        greet(lax.rem(m + i, members), s)

    @pl.when(rim_at < 5)
    def _():
        @pl.loop(0, members)
        def _(i):
            greet(i, up)

    @pl.when(jnp.logical_and(rim_at >= 5, rim_at < HOLDERS))
    def _():
        @pl.loop(0, members)
        def _(i):
            greet(i, down)

    for partners in ring:
        for slab in partners:
            greet(m, slab)

    for copy in loads:
        copy.wait()

    @pl.loop(0, ROWS)
    def _(r):
        from_row = (r // 8) * (8 * SUB) + lax.rem(r, 8)
        for i in range(3):
            for p in range(PARTS):
                a[3 * (r + RIM) + i, p] = raw[i, pl.ds(p * ROWS * SUB + from_row, SUB, stride=8)]
        bed[r + RIM, 0] = raw_bed[0, pl.ds(from_row, SUB, stride=8)]
        rough = raw_bed[1, pl.ds(from_row, SUB, stride=8)]
        bed[r + RIM, 1] = (gravity * time_step) * rough * rough

    step_rows(a, bed, 1, ROWS - 2, first, last_row, keep_in(b, RIM))
    step_rows(b, bed, 2, ROWS - 4, first, last_row, keep_in(c, 0))

    pl.semaphore_wait(barrier, members - 1 + 4 + sum(n - 1 for n in BARS) + HOLDERS)

    low, high = 3 * RIM, 3 * (RIM + ROWS)
    halos = [
        remote(bed.at[pl.ds(ROWS, RIM)], bed.at[pl.ds(0, RIM)], halo_send.at[0], halo_recv.at[0], across, down),
        remote(bed.at[pl.ds(RIM, RIM)], bed.at[pl.ds(RIM + ROWS, RIM)], halo_send.at[1], halo_recv.at[1], across, up),
        remote(a.at[pl.ds(high - 5, 5)], a.at[pl.ds(low - 5, 5)], halo_send.at[2], halo_recv.at[2], m, down),
        remote(a.at[pl.ds(low, 3)], a.at[pl.ds(high, 3)], halo_send.at[3], halo_recv.at[3], m, up),
        remote(a.at[pl.ds(low + 4, 1)], a.at[pl.ds(high + 4, 1)], halo_send.at[4], halo_recv.at[4], m, up),
    ]
    for copy in halos:
        copy.start()

    def spread(to):
        return remote(c.at[pl.ds(3 * to, 3)], held.at[m], s1.at[to], r1.at[m], to, s)

    def spread_from(source):
        return remote(c.at[pl.ds(0, 3)], held.at[source], s1.at[source], r1.at[source], source, s)

    def inner(j):
        return jnp.logical_and(j >= 2, j < ROWS - 2)

    @pl.loop(1, members)
    def _(i):
        to = lax.rem(m + i, members)

        @pl.when(inner(to))
        def _():
            spread(to).start()

    for copy in halos:
        copy.wait_recv()

    step_rows(a, bed, -1, 2, first, last_row, keep_in(b, RIM))
    step_rows(a, bed, ROWS - 1, 2, first, last_row, keep_in(b, RIM))
    step_rows(b, bed, 0, 2, first, last_row, keep_in(c, 0))
    step_rows(b, bed, ROWS - 2, 2, first, last_row, keep_in(c, 0))

    rim_slots = [3 * ROWS - 5 + i for i in range(5)] + [0, 1, 2, 4]
    rims = [
        remote(c.at[rim_slots[i]], held_rim.at[m], sh.at[i], rh.at[m], member, slab)
        for i, (member, slab) in enumerate(holder)
    ]
    for copy in rims:
        copy.start()

    @pl.loop(1, members)
    def _(i):
        to = lax.rem(m + i, members)

        @pl.when(jnp.logical_not(inner(to)))
        def _():
            spread(to).start()

    held[m] = c[pl.ds(3 * m, 3)]
    bed_copy = pltpu.make_async_copy(bed, bed_out, own_sem.at[0])
    bed_copy.start()

    cell = gauges[...] - first * (SUB * LANES)
    block = cell >> 7
    lane = cell & (LANES - 1)
    count = cell.shape[1]
    blocks = ROWS * SUB
    pick = jnp.where(
        lax.broadcasted_iota(jnp.int32, (blocks, count), 0) == block, 1.0, 0.0
    ).astype(jnp.bfloat16)
    inside = jnp.logical_and(block >= 0, block < blocks)
    here = jnp.logical_and(
        lax.broadcasted_iota(jnp.int32, (LANES, count), 0) == lane, inside
    )
    totals = []
    for p in range(PARTS):
        water = jnp.concatenate([c[3 * r + WATER, p] for r in range(ROWS)], axis=0).T
        value = jnp.zeros((LANES, count), jnp.float32)
        for _ in range(3):
            part = water.astype(jnp.bfloat16)
            value += jnp.dot(part, pick, preferred_element_type=jnp.float32)
            water = water - part.astype(jnp.float32)
        misfit = jnp.where(here, (value - observed[...]) ** 2, 0.0)
        total = jnp.sum(misfit, axis=0, keepdims=True)
        totals.append(sum(total[:, i : i + LANES] for i in range(0, count, LANES)))
    sub = lax.broadcasted_iota(jnp.int32, (8, LANES), 0)
    sums[0] = jnp.where(sub == 0, totals[0], jnp.where(sub == 1, totals[1], 0.0))

    def stage(t):
        base = sum(n - 1 for n in BARS[:t])
        return [
            remote(sums.at[t], got.at[base + i], ls.at[base + i], lr.at[base + i], m, slab)
            for i, slab in enumerate(ring[t])
        ]

    def fold(t, copies):
        base = sum(n - 1 for n in BARS[:t])
        value = sums[t]
        for i, copy in enumerate(copies):
            copy.wait_recv()
            value = value + got[base + i]
        sums[t + 1] = value

    stages = [stage(0)]
    for copy in stages[0]:
        copy.start()

    @pl.loop(1, members)
    def _(i):
        spread_from(lax.rem(m + i, members)).wait_recv()

    @pl.when(rim_at < HOLDERS)
    def _():
        @pl.loop(0, members)
        def _(i):
            remote(c.at[0], held_rim.at[i], sh.at[0], rh.at[i], i, down).wait_recv()

    def route(to):
        return remote(out.at[to], state_out.at[pl.ds(3 * (m + RIM), 3)], s2.at[to], r2.at[m], to, s)

    def route_from(source):
        return remote(out.at[source], state_out.at[pl.ds(3 * (source + RIM), 3)], s2.at[source], r2.at[source], source, s)

    def route_rim(to):
        return remote(out_rim.at[to], state_out.at[rim_slot], s2h.at[to], r2h.at[rim_at], to, s)

    def wanted(to):
        for k in range(PARTS):
            q = ancestors[PARTS * to + k]
            for f in range(3):
                out[to, f, k] = held[q // PARTS, f, lax.rem(q, PARTS)]

    def wanted_rim(to):
        for k in range(PARTS):
            q = ancestors[PARTS * to + k]
            out_rim[to, k] = held_rim[q // PARTS, lax.rem(q, PARTS)]

    @pl.loop(1, members)
    def _(i):
        to = lax.rem(m + i, members)
        wanted(to)
        route(to).start()

        @pl.when(rim_at < HOLDERS)
        def _():
            wanted_rim(to)
            route_rim(to).start()

    wanted(m)
    mine = pltpu.make_async_copy(out.at[m], state_out.at[pl.ds(3 * (m + RIM), 3)], own_sem.at[1])
    mine.start()

    @pl.when(rim_at < HOLDERS)
    def _():
        wanted_rim(m)
        pltpu.make_async_copy(out_rim.at[m], state_out.at[rim_slot], own_sem.at[2]).start()

    for t in range(len(BARS)):
        fold(t, stages[t])
        if t + 1 < len(BARS):
            stages.append(stage(t + 1))
            for copy in stages[t + 1]:
                copy.start()

    final = sums.at[len(BARS)]

    def tell(to):
        return remote(final, lik_out.at[m], ms.at[to], mr.at[m], to, s)

    @pl.loop(1, members)
    def _(i):
        tell(lax.rem(m + i, members)).start()

    mine_lik = pltpu.make_async_copy(final, lik_out.at[m], own_sem.at[3])
    mine_lik.start()

    for copy in halos + rims:
        copy.wait_send()
    for copies in stages:
        for copy in copies:
            copy.wait_send()

    @pl.loop(1, members)
    def _(i):
        to = lax.rem(m + i, members)
        spread(to).wait_send()
        route(to).wait_send()
        tell(to).wait_send()

        @pl.when(rim_at < HOLDERS)
        def _():
            route_rim(to).wait_send()

    @pl.loop(1, members)
    def _(i):
        source = lax.rem(m + i, members)
        route_from(source).wait_recv()
        remote(final, lik_out.at[source], ms.at[source], mr.at[source], source, s).wait_recv()

    for i, (member, _) in enumerate(holder):
        slot = 1 + i + 48 * (i // 5) + i // 8

        @pl.when(m != member)
        def _(i=i, slot=slot, member=member):
            remote(out_rim.at[0], state_out.at[slot], s2h.at[0], r2h.at[i], member, s).wait_recv()

    bed_copy.wait()
    mine.wait()
    mine_lik.wait()

    @pl.when(rim_at < HOLDERS)
    def _():
        pltpu.make_async_copy(out_rim.at[m], state_out.at[rim_slot], own_sem.at[2]).wait()


def finish_kernel(
    slabs, state_in, bed_in, lik_in, water_out, east_out, south_out, weight_out,
    a, b, bed, lik, done, in_sem, out_sem,
):
    m = lax.axis_index("member")
    s = lax.axis_index("space")
    first = s * ROWS
    last_row = slabs * ROWS - 1
    loads = [
        pltpu.make_async_copy(src, dst, in_sem.at[i])
        for i, (src, dst) in enumerate(((state_in, a), (bed_in, bed), (lik_in, lik)))
    ]
    for copy in loads:
        copy.start()
    for copy in loads:
        copy.wait()
    step_rows(a, bed, -1, EXT - 2, first, last_row, keep_in(b, RIM))

    def store(row, p, field, value):
        start = p * ROWS * SUB + (row // 8) * (8 * SUB) + lax.rem(row, 8)
        done[field, pl.ds(start, SUB, stride=8)] = value

    step_rows(b, bed, 0, ROWS, first, last_row, store)
    copies = [
        pltpu.make_async_copy(done.at[i], ref, out_sem.at[i])
        for i, ref in enumerate((east_out, water_out, south_out))
    ]
    for copy in copies:
        copy.start()

    total = -0.5 * jnp.sum(lik[...], axis=2, keepdims=True)
    total = jnp.broadcast_to(total, lik.shape)
    named = lax.broadcasted_iota(jnp.int32, lik.shape, 1) < PARTS
    top = jnp.max(jnp.where(named, total, -jnp.inf), axis=(0, 1), keepdims=True)
    shifted = total - top
    mass = jnp.sum(jnp.where(named, jnp.exp(jnp.where(named, shifted, 0.0)), 0.0), axis=(0, 1), keepdims=True)
    lik[...] = shifted - jnp.log(mass)
    own = lik[m]
    sub = lax.broadcasted_iota(jnp.int32, own.shape, 0)
    lane = lax.broadcasted_iota(jnp.int32, own.shape, 1)
    for p in range(PARTS):
        weight_out[p] = jnp.sum(jnp.where(jnp.logical_and(sub == p, lane == 0), own, 0.0))
    for copy in copies:
        copy.wait()


def to_blocks(x):
    lead = x.shape[:-2]
    n = len(lead)
    x = x.reshape(*lead, x.shape[-2] // 8, 8, SUB, LANES)
    x = x.transpose(*range(n), n, n + 2, n + 1, n + 3)
    return x.reshape(-1, LANES)


def from_blocks(x, parts, rows, width):
    x = x.reshape(parts, rows // 8, SUB, 8, LANES).transpose(0, 1, 3, 2, 4)
    return x.reshape(parts, rows, width)


def shards(members, slabs, depth, flow_x, flow_y, terrain, roughness, gauges, observed, ancestors):
    parts, rows, width = depth.shape
    f32 = jnp.float32
    hbm = pl.BlockSpec(memory_space=pl.ANY)
    vmem = pl.BlockSpec(memory_space=pltpu.VMEM)
    smem = pl.BlockSpec(memory_space=pltpu.SMEM)
    row = (PARTS, SUB, LANES)
    dma = pltpu.SemaphoreType.DMA
    stages = sum(n - 1 for n in BARS)
    cells = parts * rows * SUB
    state, bed, lik = pl.pallas_call(
        functools.partial(exchange_kernel, members, slabs),
        out_shape=(
            jax.ShapeDtypeStruct((3 * EXT, *row), f32),
            jax.ShapeDtypeStruct((EXT, 2, SUB, LANES), f32),
            jax.ShapeDtypeStruct((members, 8, LANES), f32),
        ),
        in_specs=[hbm] * 5 + [vmem] * 2 + [smem],
        out_specs=(hbm, hbm, hbm),
        scratch_shapes=[
            pltpu.VMEM((3, cells, LANES), f32),
            pltpu.VMEM((2, rows * SUB, LANES), f32),
            pltpu.VMEM((3 * EXT, *row), f32),
            pltpu.VMEM((3 * EXT, *row), f32),
            pltpu.VMEM((3 * ROWS, *row), f32),
            pltpu.VMEM((EXT, 2, SUB, LANES), f32),
            pltpu.VMEM((members, 3, *row), f32),
            pltpu.VMEM((members, *row), f32),
            pltpu.VMEM((members, 3, *row), f32),
            pltpu.VMEM((members, *row), f32),
            pltpu.VMEM((len(BARS) + 1, 8, LANES), f32),
            pltpu.VMEM((stages, 8, LANES), f32),
            dma((5,)),
            dma((5,)), dma((5,)),
            dma((members,)), dma((members,)),
            dma((HOLDERS,)), dma((members,)),
            dma((members,)), dma((members,)),
            dma((members,)), dma((HOLDERS,)),
            dma((stages,)), dma((stages,)),
            dma((members,)), dma((members,)),
            dma((4,)),
        ],
        compiler_params=pltpu.CompilerParams(
            collective_id=0, has_side_effects=True, vmem_limit_bytes=VMEM_LIMIT
        ),
        name="exchange",
    )(
        to_blocks(depth), to_blocks(flow_x), to_blocks(flow_y), to_blocks(terrain), to_blocks(roughness),
        gauges.reshape(1, -1), observed.reshape(1, -1), ancestors,
    )
    water, east, south, weight = pl.pallas_call(
        functools.partial(finish_kernel, slabs),
        out_shape=(jax.ShapeDtypeStruct((cells, LANES), f32),) * 3
        + (jax.ShapeDtypeStruct((parts,), f32),),
        in_specs=[hbm] * 3,
        out_specs=(hbm, hbm, hbm, smem),
        scratch_shapes=[
            pltpu.VMEM((3 * EXT, *row), f32),
            pltpu.VMEM((3 * EXT, *row), f32),
            pltpu.VMEM((EXT, 2, SUB, LANES), f32),
            pltpu.VMEM((members, 8, LANES), f32),
            pltpu.VMEM((3, cells, LANES), f32),
            dma((3,)), dma((3,)),
        ],
        compiler_params=pltpu.CompilerParams(vmem_limit_bytes=VMEM_LIMIT),
        name="finish",
    )(state, bed, lik)
    back = functools.partial(from_blocks, parts=parts, rows=rows, width=width)
    return back(water), back(east), back(south), weight


def solution(mesh):
    placed = (P("member", "space", None),) * 3 + (P("space", None),) * 2 + (P(),) * 3
    return jax.shard_map(
        functools.partial(shards, mesh.shape["member"], mesh.shape["space"]),
        mesh=mesh,
        in_specs=placed,
        out_specs=(P("member", "space", None),) * 3 + (P("member"),),
        check_vma=False,
    )
```

```python
import functools

import jax
import jax.numpy as jnp
from jax import lax
from jax.experimental import pallas as pl
from jax.experimental.pallas import tpu as pltpu
from jax.sharding import PartitionSpec as P

MESH = pl.DeviceIdType.MESH
gravity = 9.81
time_step = 1.0
cell_size = 30.0
depth_floor = 0.1

EAST, WATER, SOUTH = 0, 1, 2
ROWS = 16
LANES = 128
PARTS = 2
SUB = 16
RIM = 2
EXT = ROWS + 2 * RIM
HOLDERS = 9
VMEM_LIMIT = 60 * 2**20


def next_column(x):
    y = pltpu.roll(x, LANES - 1, 1)
    lane = lax.broadcasted_iota(jnp.int32, x.shape, 1)
    return jnp.where(lane == LANES - 1, pltpu.roll(y, SUB - 1, 0), y)


def previous_column(x):
    y = pltpu.roll(x, 1, 1)
    lane = lax.broadcasted_iota(jnp.int32, x.shape, 1)
    return jnp.where(lane == 0, pltpu.roll(y, 1, 0), y)


def face(flow, eta_a, eta_b, bed_top, friction):
    hflow = jnp.maximum(jnp.maximum(eta_a, eta_b) - bed_top, depth_floor)
    push = flow - (gravity * time_step / cell_size) * hflow * (eta_b - eta_a)
    drag = 1.0 + friction * jnp.abs(flow) * jnp.exp2(lax.log2(hflow) * (-7.0 / 3.0))
    inverse = pl.reciprocal(drag, approx=True)
    inverse = inverse * (2.0 - drag * inverse)
    return push * inverse


def south_flow(src, bed, row, first, last_row):
    at = row + RIM
    bed_a, bed_b = bed[at, 0], bed[at + 1, 0]
    bed_top = jnp.maximum(bed_a, bed_b)
    friction = bed[at, 1]
    ok = jnp.logical_and(first + row >= 0, first + row < last_row)
    out = []
    for p in range(PARTS):
        eta_a = bed_a + src[3 * at + WATER, p]
        eta_b = bed_b + src[3 * (at + 1) + WATER, p]
        flow = face(src[3 * at + SOUTH, p], eta_a, eta_b, bed_top, friction)
        out.append(jnp.where(ok, flow, 0.0))
    return tuple(out)


def step_rows(src, bed, low, count, unroll, first, last_row, store):
    sub = lax.broadcasted_iota(jnp.int32, (SUB, LANES), 0)
    lane = lax.broadcasted_iota(jnp.int32, (SUB, LANES), 1)
    rim = jnp.logical_and(sub == SUB - 1, lane == LANES - 1)

    def one(i, north):
        row = low + i
        at = row + RIM
        south = south_flow(src, bed, row, first, last_row)
        bed_a = bed[at, 0]
        bed_top = jnp.maximum(bed_a, next_column(bed_a))
        friction = bed[at, 1]
        for p in range(PARTS):
            water = src[3 * at + WATER, p]
            eta = bed_a + water
            east = face(src[3 * at + EAST, p], eta, next_column(eta), bed_top, friction)
            east = jnp.where(rim, 0.0, east)
            west = previous_column(east)
            new = water + (time_step / cell_size) * (west - east + north[p] - south[p])
            store(row, p, EAST, east)
            store(row, p, WATER, new)
            store(row, p, SOUTH, south[p])
        return south

    def some(i, north):
        for k in range(unroll):
            north = one(i * unroll + k, north)
        return north

    north = south_flow(src, bed, low - 1, first, last_row)
    if count == unroll:
        some(0, north)
    else:
        lax.fori_loop(0, count // unroll, some, north)


def keep_in(dst, rim):
    def store(row, p, field, value):
        dst[3 * (row + rim) + field, p] = value

    return store


def exchange_kernel(
    members, slabs,
    water_in, east_in, south_in, bed_in, rough_in, gauges_in, observed_in, ancestors_in,
    state_out, bed_out, lik_out,
    raw, raw_bed, a, b, c, bed, held, held_rim, out, out_rim, pick, slab_lik, sums, far_lik, own_lik,
    gauges, observed, ancestors, in_sem, halo_send, halo_recv, s1, r1, sh, rh, s2, r2, s2h, r2h, ls, lr, fs, fr, ms, mr, own_sem, here_sem,
):
    m = lax.axis_index("member")
    s = lax.axis_index("space")
    up = lax.rem(s + slabs - 1, slabs)
    down = lax.rem(s + 1, slabs)
    across = lax.rem(m + members // 2, members)
    first = s * ROWS
    last_row = slabs * ROWS - 1
    rim_at = m // 2 + 8 * lax.rem(m, 2)
    rim_slot = 1 + rim_at + 48 * (rim_at // 5) + rim_at // 8
    has_up = (s + slabs - 1) // slabs
    has_down = (2 * slabs - 2 - s) // slabs
    holder = [(2 * i if i < 8 else 1, down if i < 5 else up) for i in range(HOLDERS)]

    def remote(src, dst, send, recv, member, slab):
        return pltpu.make_async_remote_copy(
            src_ref=src, dst_ref=dst, send_sem=send, recv_sem=recv,
            device_id=(member, slab), device_id_type=MESH,
        )

    loads = [
        pltpu.make_async_copy(ref, raw.at[i], in_sem.at[i])
        for i, ref in enumerate((east_in, water_in, south_in))
    ] + [
        pltpu.make_async_copy(ref, raw_bed.at[i], in_sem.at[3 + i])
        for i, ref in enumerate((bed_in, rough_in))
    ]
    small = [
        pltpu.make_async_copy(ref, dst, in_sem.at[5 + i])
        for i, (ref, dst) in enumerate(
            ((gauges_in, gauges), (observed_in, observed), (ancestors_in, ancestors))
        )
    ]
    for copy in loads + small:
        copy.start()

    barrier = pltpu.get_barrier_semaphore()

    def greet(member, slab):
        pl.semaphore_signal(barrier, inc=1, device_id=(member, slab), device_id_type=MESH)

    for slab, there in ((up, has_up), (down, has_down)):

        @pl.when(there == 1)
        def _(slab=slab):
            greet(m, slab)
            greet(across, slab)

    @pl.loop(1, members)
    def _(i):
        greet(lax.rem(m + i, members), s)

    for copy in loads:
        copy.wait()

    def lay_out(r):
        from_row = (r // 8) * (8 * SUB) + lax.rem(r, 8)
        for i in range(3):
            for p in range(PARTS):
                a[3 * (r + RIM) + i, p] = raw[i, pl.ds(p * ROWS * SUB + from_row, SUB, stride=8)]
        bed[r + RIM, 0] = raw_bed[0, pl.ds(from_row, SUB, stride=8)]
        rough = raw_bed[1, pl.ds(from_row, SUB, stride=8)]
        bed[r + RIM, 1] = (gravity * time_step) * rough * rough

    @pl.loop(0, RIM)
    def _(r):
        lay_out(r)
        lay_out(ROWS - 1 - r)

    pl.semaphore_wait(barrier, members - 1 + 2 * (has_up + has_down))

    low, high = 3 * RIM, 3 * (RIM + ROWS)
    halos_down = [
        remote(bed.at[pl.ds(ROWS, RIM)], bed.at[pl.ds(0, RIM)], halo_send.at[0], halo_recv.at[0], across, down),
        remote(a.at[pl.ds(high - 5, 5)], a.at[pl.ds(low - 5, 5)], halo_send.at[2], halo_recv.at[2], m, down),
    ]
    halos_up = [
        remote(bed.at[pl.ds(RIM, RIM)], bed.at[pl.ds(RIM + ROWS, RIM)], halo_send.at[1], halo_recv.at[1], across, up),
        remote(a.at[pl.ds(low, 3)], a.at[pl.ds(high, 3)], halo_send.at[3], halo_recv.at[3], m, up),
        remote(a.at[pl.ds(low + 4, 1)], a.at[pl.ds(high + 4, 1)], halo_send.at[4], halo_recv.at[4], m, up),
    ]

    def toward(there, copies, act):
        @pl.when(there == 1)
        def _():
            for copy in copies:
                act(copy)

    toward(has_down, halos_down, lambda copy: copy.start())
    toward(has_up, halos_up, lambda copy: copy.start())

    def announce(t):
        @pl.when(s >= 2**t)
        def _():
            pl.semaphore_signal(here_sem.at[2 * t], inc=1, device_id=(m, s - 2**t), device_id_type=MESH)

        @pl.when(s + 2**t < slabs)
        def _():
            pl.semaphore_signal(here_sem.at[2 * t + 1], inc=1, device_id=(m, s + 2**t), device_id_type=MESH)

    def heard(t):
        @pl.when(s + 2**t < slabs)
        def _():
            pl.semaphore_wait(here_sem.at[2 * t], 1)

        @pl.when(s >= 2**t)
        def _():
            pl.semaphore_wait(here_sem.at[2 * t + 1], 1)

    announce(0)

    @pl.loop(RIM, ROWS - RIM)
    def _(r):
        lay_out(r)

    step_rows(a, bed, 1, ROWS - 2, 7, first, last_row, keep_in(b, RIM))
    step_rows(b, bed, 2, ROWS - 4, 4, first, last_row, keep_in(c, 0))

    heard(0)
    announce(1)

    def spread(to):
        return remote(c.at[pl.ds(3 * to, 3)], held.at[m], s1.at[to], r1.at[m], to, s)

    def spread_from(source):
        return remote(c.at[pl.ds(0, 3)], held.at[source], s1.at[source], r1.at[source], source, s)

    for copy in small:
        copy.wait()

    cell = gauges[...] - first * (SUB * LANES)
    block = cell >> 7
    lane = cell & (LANES - 1)
    count = cell.shape[1]
    blocks = ROWS * SUB
    pick[...] = jnp.where(
        lax.broadcasted_iota(jnp.int32, (blocks, count), 0) == block, 1.0, 0.0
    ).astype(jnp.bfloat16)
    inside = jnp.logical_and(block >= 0, block < blocks)
    here = jnp.logical_and(
        lax.broadcasted_iota(jnp.int32, (LANES, count), 0) == lane, inside
    )

    heard(1)
    announce(2)
    toward(has_up, halos_down, lambda copy: copy.wait_recv())
    toward(has_down, halos_up, lambda copy: copy.wait_recv())
    heard(2)
    announce(3)

    step_rows(a, bed, -1, 2, 2, first, last_row, keep_in(b, RIM))
    step_rows(a, bed, ROWS - 1, 2, 2, first, last_row, keep_in(b, RIM))
    step_rows(b, bed, 0, 2, 2, first, last_row, keep_in(c, 0))
    step_rows(b, bed, ROWS - 2, 2, 2, first, last_row, keep_in(c, 0))

    water = jnp.concatenate(
        [jnp.concatenate([c[3 * r + WATER, p] for r in range(ROWS)], axis=0).T for p in range(PARTS)], axis=0
    )
    value = jnp.zeros((PARTS * LANES, count), jnp.float32)
    for _ in range(3):
        part = water.astype(jnp.bfloat16)
        value += jnp.dot(part, pick[...], preferred_element_type=jnp.float32)
        water = water - part.astype(jnp.float32)
    sub = lax.broadcasted_iota(jnp.int32, (8, LANES), 0)
    at_lane = lax.broadcasted_iota(jnp.int32, (8, LANES), 1)
    tile = jnp.zeros((8, LANES), jnp.float32)
    for p in range(PARTS):
        misfit = jnp.where(here, (value[p * LANES : (p + 1) * LANES] - observed[...]) ** 2, 0.0)
        total = jnp.sum(jnp.sum(misfit, axis=0, keepdims=True), axis=1, keepdims=True)
        spot = jnp.logical_and(sub == s // 4, at_lane == 32 * lax.rem(s, 4) + PARTS * m + p)
        tile = jnp.where(spot, total, tile)
    slab_lik[m] = tile
    twin = s + 1 - 2 * lax.rem(s, 2)

    def share(to):
        return remote(slab_lik.at[m], slab_lik.at[m], ls.at[to], lr.at[m], to, s)

    def share_twin(to):
        return remote(slab_lik.at[m], slab_lik.at[members + m], ls.at[members + to], lr.at[members + m], to, twin)

    @pl.loop(0, members)
    def _(i):
        share_twin(lax.rem(m + i, members)).start()

    @pl.loop(1, members)
    def _(i):
        share(lax.rem(m + i, members)).start()

    @pl.loop(1, members)
    def _(i):
        spread(lax.rem(m + i, members)).start()

    rim_slots = [3 * ROWS - 5 + i for i in range(5)] + [0, 1, 2, 4]
    rims = [
        remote(c.at[rim_slots[i]], held_rim.at[m], sh.at[i], rh.at[m], member, slab)
        for i, (member, slab) in enumerate(holder)
    ]
    toward(has_down, rims[:5], lambda copy: copy.start())
    toward(has_up, rims[5:], lambda copy: copy.start())

    held[m] = c[pl.ds(3 * m, 3)]
    bed_copy = pltpu.make_async_copy(bed, bed_out, own_sem.at[0])
    bed_copy.start()

    def route(to):
        return remote(out.at[to], state_out.at[pl.ds(3 * (m + RIM), 3)], s2.at[to], r2.at[m], to, s)

    def route_from(source):
        return remote(out.at[source], state_out.at[pl.ds(3 * (source + RIM), 3)], s2.at[source], r2.at[source], source, s)

    def route_rim(to):
        return remote(out_rim.at[to], state_out.at[rim_slot], s2h.at[to], r2h.at[rim_at], to, s)

    def wanted(to):
        for k in range(PARTS):
            q = ancestors[PARTS * to + k]
            for f in range(3):
                out[to, f, k] = held[q // PARTS, f, lax.rem(q, PARTS)]

    def wanted_rim(to):
        for k in range(PARTS):
            q = ancestors[PARTS * to + k]
            out_rim[to, k] = held_rim[q // PARTS, lax.rem(q, PARTS)]

    def route_row():
        @pl.loop(1, members)
        def _(i):
            spread_from(lax.rem(m + i, members)).wait_recv()

        @pl.loop(1, members)
        def _(i):
            to = lax.rem(m + i, members)
            wanted(to)
            route(to).start()

        wanted(m)
        pltpu.make_async_copy(out.at[m], state_out.at[pl.ds(3 * (m + RIM), 3)], own_sem.at[1]).start()

    heard(3)
    announce(4)

    @pl.loop(0, members)
    def _(i):
        remote(slab_lik.at[i], slab_lik.at[members + i], ls.at[i], lr.at[members + i], i, twin).wait_recv()

    @pl.loop(1, members)
    def _(i):
        source = lax.rem(m + i, members)
        remote(slab_lik.at[source], slab_lik.at[source], ls.at[source], lr.at[source], source, s).wait_recv()

    tile = slab_lik[0]
    for i in range(1, 2 * members):
        tile = tile + slab_lik[i]
    sums[...] = tile
    heard(4)

    carry = remote(sums, far_lik, fs.at[0], fr.at[0], m, lax.rem(s + 2 * (m + 1), slabs))

    @pl.when(m < members - 1)
    def _():
        carry.start()

    @pl.when(m == members - 1)
    def _():
        far_lik[...] = jnp.zeros((8, LANES), jnp.float32)

    route_row()

    rim_here = jnp.logical_or(
        jnp.logical_and(rim_at < 5, has_up == 1),
        jnp.logical_and(jnp.logical_and(rim_at >= 5, rim_at < HOLDERS), has_down == 1),
    )

    @pl.when(rim_here)
    def _():
        @pl.loop(0, members)
        def _(i):
            remote(c.at[0], held_rim.at[i], sh.at[0], rh.at[i], i, down).wait_recv()

        @pl.loop(1, members)
        def _(i):
            to = lax.rem(m + i, members)
            wanted_rim(to)
            route_rim(to).start()

        wanted_rim(m)
        pltpu.make_async_copy(out_rim.at[m], state_out.at[rim_slot], own_sem.at[2]).start()

    @pl.when(m < members - 1)
    def _():
        carry.wait_recv()

    def tell(to):
        return remote(far_lik, lik_out.at[m], ms.at[to], mr.at[m], to, s)

    @pl.loop(1, members)
    def _(i):
        tell(lax.rem(m + i, members)).start()

    own_lik[...] = far_lik[...] + sums[...]
    mine_lik = pltpu.make_async_copy(own_lik, lik_out.at[m], own_sem.at[3])
    mine_lik.start()

    toward(has_down, halos_down + rims[:5], lambda copy: copy.wait_send())
    toward(has_up, halos_up + rims[5:], lambda copy: copy.wait_send())

    @pl.when(m < members - 1)
    def _():
        carry.wait_send()

    share_twin(m).wait_send()

    @pl.loop(1, members)
    def _(i):
        to = lax.rem(m + i, members)
        spread(to).wait_send()
        route(to).wait_send()
        tell(to).wait_send()
        share(to).wait_send()
        share_twin(to).wait_send()

        @pl.when(rim_here)
        def _():
            route_rim(to).wait_send()

    @pl.loop(1, members)
    def _(i):
        source = lax.rem(m + i, members)
        route_from(source).wait_recv()
        remote(far_lik, lik_out.at[source], ms.at[source], mr.at[source], source, s).wait_recv()

    for i, (member, _) in enumerate(holder):
        slot = 1 + i + 48 * (i // 5) + i // 8

        @pl.when(jnp.logical_and(m != member, (has_up if i < 5 else has_down) == 1))
        def _(i=i, slot=slot, member=member):
            remote(out_rim.at[0], state_out.at[slot], s2h.at[0], r2h.at[i], member, s).wait_recv()

    bed_copy.wait()
    pltpu.make_async_copy(out.at[m], state_out.at[pl.ds(3 * (m + RIM), 3)], own_sem.at[1]).wait()
    mine_lik.wait()

    @pl.when(rim_here)
    def _():
        pltpu.make_async_copy(out_rim.at[m], state_out.at[rim_slot], own_sem.at[2]).wait()


def finish_kernel(
    slabs, state_in, bed_in, lik_in, water_out, east_out, south_out, weight_out,
    a, b, bed, lik, done, in_sem, out_sem,
):
    m = lax.axis_index("member")
    s = lax.axis_index("space")
    first = s * ROWS
    last_row = slabs * ROWS - 1
    half = ROWS // 2
    cut = 3 * (half + 2 * RIM)
    loads = [
        pltpu.make_async_copy(bed_in, bed, in_sem.at[0]),
        pltpu.make_async_copy(state_in.at[pl.ds(0, cut)], a.at[pl.ds(0, cut)], in_sem.at[1]),
        pltpu.make_async_copy(state_in.at[pl.ds(cut, 3 * EXT - cut)], a.at[pl.ds(cut, 3 * EXT - cut)], in_sem.at[2]),
        pltpu.make_async_copy(lik_in, lik, in_sem.at[3]),
    ]
    for copy in loads:
        copy.start()

    def store(row, p, field, value):
        start = p * ROWS * SUB + (row // 8) * (8 * SUB) + lax.rem(row, 8)
        done[field, pl.ds(start, SUB, stride=8)] = value

    copies = []

    def write(part):
        for p in range(PARTS):
            at = pl.ds((2 * p + part) * half * SUB, half * SUB)
            for i, ref in enumerate((east_out, water_out, south_out)):
                copy = pltpu.make_async_copy(done.at[i, at], ref.at[at], out_sem.at[part, p, i])
                copy.start()
                copies.append(copy)

    loads[0].wait()
    loads[1].wait()
    step_rows(a, bed, -1, half + 2, 5, first, last_row, keep_in(b, RIM))
    step_rows(b, bed, 0, half, 4, first, last_row, store)
    write(0)
    loads[2].wait()
    step_rows(a, bed, half + 1, half, 4, first, last_row, keep_in(b, RIM))
    step_rows(b, bed, half, half, 4, first, last_row, store)
    write(1)
    loads[3].wait()

    tile = lik[0]
    for i in range(1, lik.shape[0]):
        tile = tile + lik[i]
    total = jnp.broadcast_to(jnp.sum(tile, axis=0, keepdims=True), tile.shape)
    total = total + pltpu.roll(total, 32, 1)
    total = -0.5 * (total + pltpu.roll(total, 64, 1))
    sub = lax.broadcasted_iota(jnp.int32, total.shape, 0)
    lane = lax.broadcasted_iota(jnp.int32, total.shape, 1)
    once = jnp.logical_and(sub == 0, lane < 32)
    shifted = total - jnp.max(total)
    mass = jnp.sum(jnp.where(once, jnp.exp(shifted), 0.0))
    weights = shifted - jnp.log(jnp.broadcast_to(mass, shifted.shape))
    for p in range(PARTS):
        weight_out[p] = jnp.sum(jnp.where(jnp.logical_and(sub == 0, lane == PARTS * m + p), weights, 0.0))
    for copy in copies:
        copy.wait()


def to_blocks(x):
    lead = x.shape[:-2]
    n = len(lead)
    x = x.reshape(*lead, x.shape[-2] // 8, 8, SUB, LANES)
    x = x.transpose(*range(n), n, n + 2, n + 1, n + 3)
    return x.reshape(-1, LANES)


def from_blocks(x, parts, rows, width):
    x = x.reshape(parts, rows // 8, SUB, 8, LANES).transpose(0, 1, 3, 2, 4)
    return x.reshape(parts, rows, width)


def shards(members, slabs, depth, flow_x, flow_y, terrain, roughness, gauges, observed, ancestors):
    parts, rows, width = depth.shape
    f32 = jnp.float32
    hbm = pl.BlockSpec(memory_space=pl.ANY)
    smem = pl.BlockSpec(memory_space=pltpu.SMEM)
    row = (PARTS, SUB, LANES)
    dma = pltpu.SemaphoreType.DMA
    steps = slabs.bit_length() - 1
    count = gauges.shape[0]
    cells = parts * rows * SUB
    state, bed, lik = pl.pallas_call(
        functools.partial(exchange_kernel, members, slabs),
        out_shape=(
            jax.ShapeDtypeStruct((3 * EXT, *row), f32),
            jax.ShapeDtypeStruct((EXT, 2, SUB, LANES), f32),
            jax.ShapeDtypeStruct((members, 8, LANES), f32),
        ),
        in_specs=[hbm] * 8,
        out_specs=(hbm, hbm, hbm),
        scratch_shapes=[
            pltpu.VMEM((3, cells, LANES), f32),
            pltpu.VMEM((2, rows * SUB, LANES), f32),
            pltpu.VMEM((3 * EXT, *row), f32),
            pltpu.VMEM((3 * EXT, *row), f32),
            pltpu.VMEM((3 * ROWS, *row), f32),
            pltpu.VMEM((EXT, 2, SUB, LANES), f32),
            pltpu.VMEM((members, 3, *row), f32),
            pltpu.VMEM((members, *row), f32),
            pltpu.VMEM((members, 3, *row), f32),
            pltpu.VMEM((members, *row), f32),
            pltpu.VMEM((rows * SUB, count), jnp.bfloat16),
            pltpu.VMEM((2 * members, 8, LANES), f32),
            pltpu.VMEM((8, LANES), f32),
            pltpu.VMEM((8, LANES), f32),
            pltpu.VMEM((8, LANES), f32),
            pltpu.VMEM((1, count), jnp.int32),
            pltpu.VMEM((1, count), f32),
            pltpu.SMEM((members * PARTS,), jnp.int32),
            dma((8,)),
            dma((5,)), dma((5,)),
            dma((members,)), dma((members,)),
            dma((HOLDERS,)), dma((members,)),
            dma((members,)), dma((members,)),
            dma((members,)), dma((HOLDERS,)),
            dma((2 * members,)), dma((2 * members,)),
            dma((1,)), dma((1,)),
            dma((members,)), dma((members,)),
            dma((4,)),
            pltpu.SemaphoreType.REGULAR((2 * steps,)),
        ],
        compiler_params=pltpu.CompilerParams(
            collective_id=0, has_side_effects=True, vmem_limit_bytes=VMEM_LIMIT
        ),
        name="exchange",
    )(
        to_blocks(depth), to_blocks(flow_x), to_blocks(flow_y), to_blocks(terrain), to_blocks(roughness),
        gauges.reshape(1, -1), observed.reshape(1, -1), ancestors,
    )
    water, east, south, weight = pl.pallas_call(
        functools.partial(finish_kernel, slabs),
        out_shape=(jax.ShapeDtypeStruct((cells, LANES), f32),) * 3
        + (jax.ShapeDtypeStruct((parts,), f32),),
        in_specs=[hbm] * 3,
        out_specs=(hbm, hbm, hbm, smem),
        scratch_shapes=[
            pltpu.VMEM((3 * EXT, *row), f32),
            pltpu.VMEM((3 * EXT, *row), f32),
            pltpu.VMEM((EXT, 2, SUB, LANES), f32),
            pltpu.VMEM((members, 8, LANES), f32),
            pltpu.VMEM((3, cells, LANES), f32),
            dma((4,)), dma((2, PARTS, 3)),
        ],
        compiler_params=pltpu.CompilerParams(vmem_limit_bytes=VMEM_LIMIT),
        name="finish",
    )(state, bed, lik)
    back = functools.partial(from_blocks, parts=parts, rows=rows, width=width)
    return back(water), back(east), back(south), weight


def solution(mesh):
    placed = (P("member", "space", None),) * 3 + (P("space", None),) * 2 + (P(),) * 3
    return jax.shard_map(
        functools.partial(shards, mesh.shape["member"], mesh.shape["space"]),
        mesh=mesh,
        in_specs=placed,
        out_specs=(P("member", "space", None),) * 3 + (P("member"),),
        check_vma=False,
    )
```

```python
import functools

import jax
import jax.numpy as jnp
from jax import lax
from jax.experimental import pallas as pl
from jax.experimental.pallas import tpu as pltpu
from jax.sharding import PartitionSpec as P

MESH = pl.DeviceIdType.MESH
gravity = 9.81
time_step = 1.0
cell_size = 30.0
depth_floor = 0.1

EAST, WATER, SOUTH = 0, 1, 2
ROWS = 16
LANES = 128
PARTS = 2
SUB = 16
RIM = 2
EXT = ROWS + 2 * RIM
HOLDERS = 9
VMEM_LIMIT = 60 * 2**20


def next_column(x):
    y = pltpu.roll(x, LANES - 1, 1)
    lane = lax.broadcasted_iota(jnp.int32, x.shape, 1)
    return jnp.where(lane == LANES - 1, pltpu.roll(y, SUB - 1, 0), y)


def previous_column(x):
    y = pltpu.roll(x, 1, 1)
    lane = lax.broadcasted_iota(jnp.int32, x.shape, 1)
    return jnp.where(lane == 0, pltpu.roll(y, 1, 0), y)


def face(flow, eta_a, eta_b, bed_top, friction):
    hflow = jnp.maximum(jnp.maximum(eta_a, eta_b) - bed_top, depth_floor)
    push = flow - (gravity * time_step / cell_size) * hflow * (eta_b - eta_a)
    drag = 1.0 + friction * jnp.abs(flow) * jnp.exp2(lax.log2(hflow) * (-7.0 / 3.0))
    inverse = pl.reciprocal(drag, approx=True)
    inverse = inverse * (2.0 - drag * inverse)
    return push * inverse


def south_flow(src, bed, row, first, last_row):
    at = row + RIM
    bed_a, bed_b = bed[at, 0], bed[at + 1, 0]
    bed_top = jnp.maximum(bed_a, bed_b)
    friction = bed[at, 1]
    ok = jnp.logical_and(first + row >= 0, first + row < last_row)
    out = []
    for p in range(PARTS):
        eta_a = bed_a + src[3 * at + WATER, p]
        eta_b = bed_b + src[3 * (at + 1) + WATER, p]
        flow = face(src[3 * at + SOUTH, p], eta_a, eta_b, bed_top, friction)
        out.append(jnp.where(ok, flow, 0.0))
    return tuple(out)


def step_rows(src, bed, low, count, unroll, first, last_row, store):
    sub = lax.broadcasted_iota(jnp.int32, (SUB, LANES), 0)
    lane = lax.broadcasted_iota(jnp.int32, (SUB, LANES), 1)
    rim = jnp.logical_and(sub == SUB - 1, lane == LANES - 1)

    def one(i, north):
        row = low + i
        at = row + RIM
        south = south_flow(src, bed, row, first, last_row)
        bed_a = bed[at, 0]
        bed_top = jnp.maximum(bed_a, next_column(bed_a))
        friction = bed[at, 1]
        for p in range(PARTS):
            water = src[3 * at + WATER, p]
            eta = bed_a + water
            east = face(src[3 * at + EAST, p], eta, next_column(eta), bed_top, friction)
            east = jnp.where(rim, 0.0, east)
            west = previous_column(east)
            new = water + (time_step / cell_size) * (west - east + north[p] - south[p])
            store(row, p, EAST, east)
            store(row, p, WATER, new)
            store(row, p, SOUTH, south[p])
        return south

    def some(i, north):
        for k in range(unroll):
            north = one(i * unroll + k, north)
        return north

    north = south_flow(src, bed, low - 1, first, last_row)
    if count == unroll:
        some(0, north)
    else:
        lax.fori_loop(0, count // unroll, some, north)


def keep_in(dst, rim):
    def store(row, p, field, value):
        dst[3 * (row + rim) + field, p] = value

    return store


def exchange_kernel(
    members, slabs,
    water_in, east_in, south_in, bed_in, rough_in, gauges_in, observed_in, ancestors_in,
    state_out, bed_out, lik_out,
    raw, raw_bed, a, b, c, bed, held_a, held_b, held_c, held_rim, out, out_rim, pick, slab_lik, sums, far_lik,
    gauges, observed, ancestors, in_sem, halo_send, halo_recv, s1, r1, sh, rh, s2, r2, s2h, r2h, ls, lr, fs, fr, ms, mr, own_sem, here_sem,
):
    m = lax.axis_index("member")
    s = lax.axis_index("space")
    up = lax.rem(s + slabs - 1, slabs)
    down = lax.rem(s + 1, slabs)
    across = lax.rem(m + members // 2, members)
    first = s * ROWS
    last_row = slabs * ROWS - 1
    rim_at = m // 2 + 8 * lax.rem(m, 2)
    rim_slot = 1 + rim_at + 48 * (rim_at // 5) + rim_at // 8
    held = (held_a, held_b, held_c)
    has_up = (s + slabs - 1) // slabs
    has_down = (2 * slabs - 2 - s) // slabs
    holder = [(2 * i if i < 8 else 1, down if i < 5 else up) for i in range(HOLDERS)]

    def remote(src, dst, send, recv, member, slab):
        return pltpu.make_async_remote_copy(
            src_ref=src, dst_ref=dst, send_sem=send, recv_sem=recv,
            device_id=(member, slab), device_id_type=MESH,
        )

    loads = [
        pltpu.make_async_copy(ref, raw.at[i], in_sem.at[i])
        for i, ref in enumerate((east_in, water_in, south_in))
    ] + [
        pltpu.make_async_copy(ref, raw_bed.at[i], in_sem.at[3 + i])
        for i, ref in enumerate((bed_in, rough_in))
    ]
    small = [
        pltpu.make_async_copy(ref, dst, in_sem.at[5 + i])
        for i, (ref, dst) in enumerate(
            ((gauges_in, gauges), (observed_in, observed), (ancestors_in, ancestors))
        )
    ]
    for copy in loads + small:
        copy.start()

    barrier = pltpu.get_barrier_semaphore()

    def greet(member, slab):
        pl.semaphore_signal(barrier, inc=1, device_id=(member, slab), device_id_type=MESH)

    for slab, there in ((up, has_up), (down, has_down)):

        @pl.when(there == 1)
        def _(slab=slab):
            greet(m, slab)
            greet(across, slab)

    @pl.loop(1, members)
    def _(i):
        greet(lax.rem(m + i, members), s)

    for copy in loads:
        copy.wait()

    def lay_out(r):
        from_row = (r // 8) * (8 * SUB) + lax.rem(r, 8)
        for i in range(3):
            for p in range(PARTS):
                a[3 * (r + RIM) + i, p] = raw[i, pl.ds(p * ROWS * SUB + from_row, SUB, stride=8)]
        bed[r + RIM, 0] = raw_bed[0, pl.ds(from_row, SUB, stride=8)]
        rough = raw_bed[1, pl.ds(from_row, SUB, stride=8)]
        bed[r + RIM, 1] = (gravity * time_step) * rough * rough

    @pl.loop(0, RIM)
    def _(r):
        lay_out(r)
        lay_out(ROWS - 1 - r)

    pl.semaphore_wait(barrier, members - 1 + 2 * (has_up + has_down))

    low, high = 3 * RIM, 3 * (RIM + ROWS)
    halos_down = [
        remote(bed.at[pl.ds(ROWS, RIM)], bed.at[pl.ds(0, RIM)], halo_send.at[0], halo_recv.at[0], across, down),
        remote(a.at[pl.ds(high - 5, 5)], a.at[pl.ds(low - 5, 5)], halo_send.at[2], halo_recv.at[2], m, down),
    ]
    halos_up = [
        remote(bed.at[pl.ds(RIM, RIM)], bed.at[pl.ds(RIM + ROWS, RIM)], halo_send.at[1], halo_recv.at[1], across, up),
        remote(a.at[pl.ds(low, 3)], a.at[pl.ds(high, 3)], halo_send.at[3], halo_recv.at[3], m, up),
        remote(a.at[pl.ds(low + 4, 1)], a.at[pl.ds(high + 4, 1)], halo_send.at[4], halo_recv.at[4], m, up),
    ]

    def toward(there, copies, act):
        @pl.when(there == 1)
        def _():
            for copy in copies:
                act(copy)

    toward(has_down, halos_down, lambda copy: copy.start())
    toward(has_up, halos_up, lambda copy: copy.start())

    def announce(t):
        @pl.when(s >= 2**t)
        def _():
            pl.semaphore_signal(here_sem.at[2 * t], inc=1, device_id=(m, s - 2**t), device_id_type=MESH)

        @pl.when(s + 2**t < slabs)
        def _():
            pl.semaphore_signal(here_sem.at[2 * t + 1], inc=1, device_id=(m, s + 2**t), device_id_type=MESH)

    def heard(t):
        @pl.when(s + 2**t < slabs)
        def _():
            pl.semaphore_wait(here_sem.at[2 * t], 1)

        @pl.when(s >= 2**t)
        def _():
            pl.semaphore_wait(here_sem.at[2 * t + 1], 1)

    announce(0)

    @pl.loop(RIM, ROWS - RIM)
    def _(r):
        lay_out(r)

    step_rows(a, bed, 1, ROWS - 2, 7, first, last_row, keep_in(b, RIM))
    step_rows(b, bed, 2, ROWS - 4, 4, first, last_row, keep_in(c, 0))

    heard(0)
    announce(1)

    def spread(to, f):
        return remote(c.at[3 * to + f], held[f].at[m], s1.at[f, to], r1.at[f, m], to, s)

    def spread_from(source, f):
        return remote(c.at[f], held[f].at[source], s1.at[f, source], r1.at[f, source], source, s)

    for copy in small:
        copy.wait()

    cell = gauges[...] - first * (SUB * LANES)
    block = cell >> 7
    lane = cell & (LANES - 1)
    count = cell.shape[1]
    blocks = ROWS * SUB
    pick[...] = jnp.where(
        lax.broadcasted_iota(jnp.int32, (blocks, count), 0) == block, 1.0, 0.0
    ).astype(jnp.bfloat16)
    inside = jnp.logical_and(block >= 0, block < blocks)
    here = jnp.logical_and(
        lax.broadcasted_iota(jnp.int32, (LANES, count), 0) == lane, inside
    )

    heard(1)
    announce(2)
    heard(2)
    announce(3)
    toward(has_up, halos_down, lambda copy: copy.wait_recv())
    toward(has_down, halos_up, lambda copy: copy.wait_recv())

    step_rows(a, bed, -1, 2, 2, first, last_row, keep_in(b, RIM))
    step_rows(a, bed, ROWS - 1, 2, 2, first, last_row, keep_in(b, RIM))
    step_rows(b, bed, 0, 2, 2, first, last_row, keep_in(c, 0))
    step_rows(b, bed, ROWS - 2, 2, 2, first, last_row, keep_in(c, 0))

    water = jnp.concatenate(
        [jnp.concatenate([c[3 * r + WATER, p] for r in range(ROWS)], axis=0).T for p in range(PARTS)], axis=0
    )
    value = jnp.zeros((PARTS * LANES, count), jnp.float32)
    for _ in range(3):
        part = water.astype(jnp.bfloat16)
        value += jnp.dot(part, pick[...], preferred_element_type=jnp.float32)
        water = water - part.astype(jnp.float32)
    at_lane = lax.broadcasted_iota(jnp.int32, (1, LANES), 1)
    entry = jnp.zeros((1, LANES), jnp.float32)
    for p in range(PARTS):
        misfit = jnp.where(here, (value[p * LANES : (p + 1) * LANES] - observed[...]) ** 2, 0.0)
        total = jnp.sum(jnp.sum(misfit, axis=0, keepdims=True), axis=1, keepdims=True)
        entry = jnp.where(at_lane == 32 * lax.rem(s, 4) + PARTS * m + p, total, entry)
    slab_lik[m] = entry
    twin = s + 1 - 2 * lax.rem(s, 2)

    def share(to):
        return remote(slab_lik.at[m], slab_lik.at[m], ls.at[to], lr.at[m], to, s)

    def share_twin(to):
        return remote(slab_lik.at[m], slab_lik.at[members + m], ls.at[members + to], lr.at[members + m], to, twin)

    @pl.loop(0, members)
    def _(i):
        share_twin(lax.rem(m + i, members)).start()

    @pl.loop(1, members)
    def _(i):
        share(lax.rem(m + i, members)).start()

    def send_field(f):
        @pl.loop(1, members)
        def _(i):
            spread(lax.rem(m + i, members), f).start()

    send_field(0)

    rim_slots = [3 * ROWS - 5 + i for i in range(5)] + [0, 1, 2, 4]
    rims = [
        remote(c.at[rim_slots[i]], held_rim.at[m], sh.at[i], rh.at[m], member, slab)
        for i, (member, slab) in enumerate(holder)
    ]
    toward(has_down, rims[:5], lambda copy: copy.start())
    toward(has_up, rims[5:], lambda copy: copy.start())

    send_field(1)
    send_field(2)
    for f in range(3):
        held[f][m] = c[3 * m + f]
    bed_copy = pltpu.make_async_copy(bed, bed_out, own_sem.at[6])
    bed_copy.start()

    def route(to, f):
        return remote(out.at[to, f], state_out.at[3 * (m + RIM) + f], s2.at[f, to], r2.at[f, m], to, s)

    def route_from(source, f):
        return remote(out.at[source, f], state_out.at[3 * (source + RIM) + f], s2.at[f, source], r2.at[f, source], source, s)

    def route_rim(to):
        return remote(out_rim.at[to], state_out.at[rim_slot], s2h.at[to], r2h.at[rim_at], to, s)

    def wanted(to, f):
        for k in range(PARTS):
            q = ancestors[PARTS * to + k]
            out[to, f, k] = held[f][q // PARTS, lax.rem(q, PARTS)]

    def wanted_rim(to):
        for k in range(PARTS):
            q = ancestors[PARTS * to + k]
            out_rim[to, k] = held_rim[q // PARTS, lax.rem(q, PARTS)]

    def mine(f):
        return pltpu.make_async_copy(out.at[m, f], state_out.at[3 * (m + RIM) + f], own_sem.at[f])

    def route_field(f):
        @pl.loop(1, members)
        def _(i):
            spread_from(lax.rem(m + i, members), f).wait_recv()

        @pl.loop(1, members)
        def _(i):
            to = lax.rem(m + i, members)
            wanted(to, f)
            route(to, f).start()

        wanted(m, f)
        mine(f).start()

    heard(3)
    announce(4)

    carry = remote(sums, far_lik, fs.at[0], fr.at[0], m, lax.rem(s + 2 * (m + 1), slabs))

    def carry_sums():
        @pl.loop(0, members)
        def _(i):
            remote(slab_lik.at[i], slab_lik.at[members + i], ls.at[i], lr.at[members + i], i, twin).wait_recv()

        @pl.loop(1, members)
        def _(i):
            source = lax.rem(m + i, members)
            remote(slab_lik.at[source], slab_lik.at[source], ls.at[source], lr.at[source], source, s).wait_recv()

        entry = slab_lik[0]
        for i in range(1, 2 * members):
            entry = entry + slab_lik[i]
        sums[...] = entry
        heard(4)

        @pl.when(m < members - 1)
        def _():
            carry.start()

    @pl.when(s >= slabs // 2)
    def _():
        carry_sums()

    route_field(0)

    @pl.when(s < slabs // 2)
    def _():
        carry_sums()

    route_field(1)
    route_field(2)

    rim_here = jnp.logical_or(
        jnp.logical_and(rim_at < 5, has_up == 1),
        jnp.logical_and(jnp.logical_and(rim_at >= 5, rim_at < HOLDERS), has_down == 1),
    )

    @pl.when(rim_here)
    def _():
        @pl.loop(0, members)
        def _(i):
            remote(c.at[0], held_rim.at[i], sh.at[0], rh.at[i], i, down).wait_recv()

        @pl.loop(1, members)
        def _(i):
            to = lax.rem(m + i, members)
            wanted_rim(to)
            route_rim(to).start()

        wanted_rim(m)
        pltpu.make_async_copy(out_rim.at[m], state_out.at[rim_slot], own_sem.at[3]).start()

    def tell(to):
        return remote(far_lik, lik_out.at[m], ms.at[to], mr.at[m], to, s)

    @pl.when(m < members - 1)
    def _():
        carry.wait_recv()

        @pl.loop(1, members)
        def _(i):
            tell(lax.rem(m + i, members)).start()

        pltpu.make_async_copy(far_lik, lik_out.at[m], own_sem.at[4]).start()

    mine_lik = pltpu.make_async_copy(sums, lik_out.at[members - 1], own_sem.at[5])
    mine_lik.start()

    toward(has_down, halos_down + rims[:5], lambda copy: copy.wait_send())
    toward(has_up, halos_up + rims[5:], lambda copy: copy.wait_send())

    @pl.when(m < members - 1)
    def _():
        carry.wait_send()
        pltpu.make_async_copy(far_lik, lik_out.at[m], own_sem.at[4]).wait()

        @pl.loop(1, members)
        def _(i):
            tell(lax.rem(m + i, members)).wait_send()

    share_twin(m).wait_send()

    @pl.loop(1, members)
    def _(i):
        to = lax.rem(m + i, members)
        for f in range(3):
            spread(to, f).wait_send()
            route(to, f).wait_send()
        share(to).wait_send()
        share_twin(to).wait_send()

        @pl.when(rim_here)
        def _():
            route_rim(to).wait_send()

    @pl.loop(1, members)
    def _(i):
        source = lax.rem(m + i, members)
        for f in range(3):
            route_from(source, f).wait_recv()

        @pl.when(source < members - 1)
        def _():
            remote(far_lik, lik_out.at[source], ms.at[source], mr.at[source], source, s).wait_recv()

    for i, (member, _) in enumerate(holder):
        slot = 1 + i + 48 * (i // 5) + i // 8

        @pl.when(jnp.logical_and(m != member, (has_up if i < 5 else has_down) == 1))
        def _(i=i, slot=slot, member=member):
            remote(out_rim.at[0], state_out.at[slot], s2h.at[0], r2h.at[i], member, s).wait_recv()

    bed_copy.wait()
    for f in range(3):
        mine(f).wait()
    mine_lik.wait()

    @pl.when(rim_here)
    def _():
        pltpu.make_async_copy(out_rim.at[m], state_out.at[rim_slot], own_sem.at[3]).wait()


def finish_kernel(
    slabs, state_in, bed_in, lik_in, water_out, east_out, south_out, weight_out,
    a, b, bed, lik, done, in_sem, out_sem,
):
    m = lax.axis_index("member")
    s = lax.axis_index("space")
    first = s * ROWS
    last_row = slabs * ROWS - 1
    half = ROWS // 2
    cut = 3 * (half + 2 * RIM)
    loads = [
        pltpu.make_async_copy(bed_in, bed, in_sem.at[0]),
        pltpu.make_async_copy(state_in.at[pl.ds(0, cut)], a.at[pl.ds(0, cut)], in_sem.at[1]),
        pltpu.make_async_copy(state_in.at[pl.ds(cut, 3 * EXT - cut)], a.at[pl.ds(cut, 3 * EXT - cut)], in_sem.at[2]),
        pltpu.make_async_copy(lik_in, lik, in_sem.at[3]),
    ]
    for copy in loads:
        copy.start()

    def store(row, p, field, value):
        start = p * ROWS * SUB + (row // 8) * (8 * SUB) + lax.rem(row, 8)
        done[field, pl.ds(start, SUB, stride=8)] = value

    copies = []

    def write(part):
        for p in range(PARTS):
            at = pl.ds((2 * p + part) * half * SUB, half * SUB)
            for i, ref in enumerate((east_out, water_out, south_out)):
                copy = pltpu.make_async_copy(done.at[i, at], ref.at[at], out_sem.at[part, p, i])
                copy.start()
                copies.append(copy)

    loads[0].wait()
    loads[1].wait()
    step_rows(a, bed, -1, half + 2, 5, first, last_row, keep_in(b, RIM))
    step_rows(b, bed, 0, half, 4, first, last_row, store)
    write(0)
    loads[2].wait()
    step_rows(a, bed, half + 1, half, 4, first, last_row, keep_in(b, RIM))
    step_rows(b, bed, half, half, 4, first, last_row, store)
    write(1)
    loads[3].wait()

    members = lik.shape[0]
    at_slab = lax.broadcasted_iota(jnp.int32, (8, LANES), 0)
    tile = jnp.zeros((8, LANES), jnp.float32)
    for i in range(members):
        source = lax.rem(s + 2 * slabs - 2 * (i + 1), slabs)
        tile = tile + jnp.where(at_slab == source // 4, lik[i], 0.0)
    total = jnp.broadcast_to(jnp.sum(tile, axis=0, keepdims=True), tile.shape)
    total = total + pltpu.roll(total, 32, 1)
    total = -0.5 * (total + pltpu.roll(total, 64, 1))
    sub = lax.broadcasted_iota(jnp.int32, total.shape, 0)
    lane = lax.broadcasted_iota(jnp.int32, total.shape, 1)
    once = jnp.logical_and(sub == 0, lane < 32)
    shifted = total - jnp.max(total)
    mass = jnp.sum(jnp.where(once, jnp.exp(shifted), 0.0))
    weights = shifted - jnp.log(jnp.broadcast_to(mass, shifted.shape))
    for p in range(PARTS):
        weight_out[p] = jnp.sum(jnp.where(jnp.logical_and(sub == 0, lane == PARTS * m + p), weights, 0.0))
    for copy in copies:
        copy.wait()


def to_blocks(x):
    lead = x.shape[:-2]
    n = len(lead)
    x = x.reshape(*lead, x.shape[-2] // 8, 8, SUB, LANES)
    x = x.transpose(*range(n), n, n + 2, n + 1, n + 3)
    return x.reshape(-1, LANES)


def from_blocks(x, parts, rows, width):
    x = x.reshape(parts, rows // 8, SUB, 8, LANES).transpose(0, 1, 3, 2, 4)
    return x.reshape(parts, rows, width)


def shards(members, slabs, depth, flow_x, flow_y, terrain, roughness, gauges, observed, ancestors):
    parts, rows, width = depth.shape
    f32 = jnp.float32
    hbm = pl.BlockSpec(memory_space=pl.ANY)
    smem = pl.BlockSpec(memory_space=pltpu.SMEM)
    row = (PARTS, SUB, LANES)
    dma = pltpu.SemaphoreType.DMA
    steps = slabs.bit_length() - 1
    count = gauges.shape[0]
    cells = parts * rows * SUB
    state, bed, lik = pl.pallas_call(
        functools.partial(exchange_kernel, members, slabs),
        out_shape=(
            jax.ShapeDtypeStruct((3 * EXT, *row), f32),
            jax.ShapeDtypeStruct((EXT, 2, SUB, LANES), f32),
            jax.ShapeDtypeStruct((members, 1, LANES), f32),
        ),
        in_specs=[hbm] * 8,
        out_specs=(hbm, hbm, hbm),
        scratch_shapes=[
            pltpu.VMEM((3, cells, LANES), f32),
            pltpu.VMEM((2, rows * SUB, LANES), f32),
            pltpu.VMEM((3 * EXT, *row), f32),
            pltpu.VMEM((3 * EXT, *row), f32),
            pltpu.VMEM((3 * ROWS, *row), f32),
            pltpu.VMEM((EXT, 2, SUB, LANES), f32),
            pltpu.VMEM((members, *row), f32),
            pltpu.VMEM((members, *row), f32),
            pltpu.VMEM((members, *row), f32),
            pltpu.VMEM((members, *row), f32),
            pltpu.VMEM((members, 3, *row), f32),
            pltpu.VMEM((members, *row), f32),
            pltpu.VMEM((rows * SUB, count), jnp.bfloat16),
            pltpu.VMEM((2 * members, 1, LANES), f32),
            pltpu.VMEM((1, LANES), f32),
            pltpu.VMEM((1, LANES), f32),
            pltpu.VMEM((1, count), jnp.int32),
            pltpu.VMEM((1, count), f32),
            pltpu.SMEM((members * PARTS,), jnp.int32),
            dma((8,)),
            dma((5,)), dma((5,)),
            dma((3, members)), dma((3, members)),
            dma((HOLDERS,)), dma((members,)),
            dma((3, members)), dma((3, members)),
            dma((members,)), dma((HOLDERS,)),
            dma((2 * members,)), dma((2 * members,)),
            dma((1,)), dma((1,)),
            dma((members,)), dma((members,)),
            dma((7,)),
            pltpu.SemaphoreType.REGULAR((2 * steps,)),
        ],
        compiler_params=pltpu.CompilerParams(
            collective_id=0, has_side_effects=True, vmem_limit_bytes=VMEM_LIMIT
        ),
        name="exchange",
    )(
        to_blocks(depth), to_blocks(flow_x), to_blocks(flow_y), to_blocks(terrain), to_blocks(roughness),
        gauges.reshape(1, -1), observed.reshape(1, -1), ancestors,
    )
    water, east, south, weight = pl.pallas_call(
        functools.partial(finish_kernel, slabs),
        out_shape=(jax.ShapeDtypeStruct((cells, LANES), f32),) * 3
        + (jax.ShapeDtypeStruct((parts,), f32),),
        in_specs=[hbm] * 3,
        out_specs=(hbm, hbm, hbm, smem),
        scratch_shapes=[
            pltpu.VMEM((3 * EXT, *row), f32),
            pltpu.VMEM((3 * EXT, *row), f32),
            pltpu.VMEM((EXT, 2, SUB, LANES), f32),
            pltpu.VMEM((members, 1, LANES), f32),
            pltpu.VMEM((3, cells, LANES), f32),
            dma((4,)), dma((2, PARTS, 3)),
        ],
        compiler_params=pltpu.CompilerParams(vmem_limit_bytes=VMEM_LIMIT),
        name="finish",
    )(state, bed, lik)
    back = functools.partial(from_blocks, parts=parts, rows=rows, width=width)
    return back(water), back(east), back(south), weight


def solution(mesh):
    placed = (P("member", "space", None),) * 3 + (P("space", None),) * 2 + (P(),) * 3
    return jax.shard_map(
        functools.partial(shards, mesh.shape["member"], mesh.shape["space"]),
        mesh=mesh,
        in_specs=placed,
        out_specs=(P("member", "space", None),) * 3 + (P("member"),),
        check_vma=False,
    )
```

```python
import functools

import jax
import jax.numpy as jnp
from jax import lax
from jax.experimental import pallas as pl
from jax.experimental.pallas import tpu as pltpu
from jax.sharding import PartitionSpec as P

MESH = pl.DeviceIdType.MESH
gravity = 9.81
time_step = 1.0
cell_size = 30.0
depth_floor = 0.1

EAST, WATER, SOUTH = 0, 1, 2
ROWS = 16
LANES = 128
PARTS = 2
SUB = 16
RIM = 2
EXT = ROWS + 2 * RIM
HOLDERS = 9
VMEM_LIMIT = 60 * 2**20


def next_column(x):
    y = pltpu.roll(x, LANES - 1, 1)
    lane = lax.broadcasted_iota(jnp.int32, x.shape, 1)
    return jnp.where(lane == LANES - 1, pltpu.roll(y, SUB - 1, 0), y)


def previous_column(x):
    y = pltpu.roll(x, 1, 1)
    lane = lax.broadcasted_iota(jnp.int32, x.shape, 1)
    return jnp.where(lane == 0, pltpu.roll(y, 1, 0), y)


def face(flow, eta_a, eta_b, bed_top, friction):
    hflow = jnp.maximum(jnp.maximum(eta_a, eta_b) - bed_top, depth_floor)
    push = flow - (gravity * time_step / cell_size) * hflow * (eta_b - eta_a)
    drag = 1.0 + friction * jnp.abs(flow) * jnp.exp2(lax.log2(hflow) * (-7.0 / 3.0))
    inverse = pl.reciprocal(drag, approx=True)
    inverse = inverse * (2.0 - drag * inverse)
    return push * inverse


def south_flow(src, bed, row, first, last_row):
    at = row + RIM
    bed_a, bed_b = bed[at, 0], bed[at + 1, 0]
    bed_top = jnp.maximum(bed_a, bed_b)
    friction = bed[at, 1]
    ok = jnp.logical_and(first + row >= 0, first + row < last_row)
    out = []
    for p in range(PARTS):
        eta_a = bed_a + src[3 * at + WATER, p]
        eta_b = bed_b + src[3 * (at + 1) + WATER, p]
        flow = face(src[3 * at + SOUTH, p], eta_a, eta_b, bed_top, friction)
        out.append(jnp.where(ok, flow, 0.0))
    return tuple(out)


def step_rows(src, bed, low, count, unroll, first, last_row, store):
    sub = lax.broadcasted_iota(jnp.int32, (SUB, LANES), 0)
    lane = lax.broadcasted_iota(jnp.int32, (SUB, LANES), 1)
    rim = jnp.logical_and(sub == SUB - 1, lane == LANES - 1)

    def one(i, north):
        row = low + i
        at = row + RIM
        south = south_flow(src, bed, row, first, last_row)
        bed_a = bed[at, 0]
        bed_top = jnp.maximum(bed_a, next_column(bed_a))
        friction = bed[at, 1]
        for p in range(PARTS):
            water = src[3 * at + WATER, p]
            eta = bed_a + water
            east = face(src[3 * at + EAST, p], eta, next_column(eta), bed_top, friction)
            east = jnp.where(rim, 0.0, east)
            west = previous_column(east)
            new = water + (time_step / cell_size) * (west - east + north[p] - south[p])
            store(row, p, EAST, east)
            store(row, p, WATER, new)
            store(row, p, SOUTH, south[p])
        return south

    def some(i, north):
        for k in range(unroll):
            north = one(i * unroll + k, north)
        return north

    north = south_flow(src, bed, low - 1, first, last_row)
    if count == unroll:
        some(0, north)
    else:
        lax.fori_loop(0, count // unroll, some, north)


def keep_in(dst, rim):
    def store(row, p, field, value):
        dst[3 * (row + rim) + field, p] = value

    return store


def exchange_kernel(
    members, slabs,
    water_in, east_in, south_in, bed_in, rough_in, gauges_in, observed_in, ancestors_in,
    state_out, bed_out, lik_out,
    raw, raw_bed, a, b, c, bed, held_a, held_b, held_c, held_rim, out, out_rim, pick, z_lik, sums,
    gauges, observed, ancestors, in_sem, halo_send, halo_recv, s1, r1, sh, rh, s2, r2, s2h, r2h, ls, lr, ms, mr, own_sem, here_sem,
):
    m = lax.axis_index("member")
    s = lax.axis_index("space")
    up = lax.rem(s + slabs - 1, slabs)
    down = lax.rem(s + 1, slabs)
    across = lax.rem(m + members // 2, members)
    first = s * ROWS
    last_row = slabs * ROWS - 1
    rim_at = m // 2 + 8 * lax.rem(m, 2)
    rim_slot = 1 + rim_at + 48 * (rim_at // 5) + rim_at // 8
    held = (held_a, held_b, held_c)
    has_up = (s + slabs - 1) // slabs
    has_down = (2 * slabs - 2 - s) // slabs
    holder = [(2 * i if i < 8 else 1, down if i < 5 else up) for i in range(HOLDERS)]

    def remote(src, dst, send, recv, member, slab):
        return pltpu.make_async_remote_copy(
            src_ref=src, dst_ref=dst, send_sem=send, recv_sem=recv,
            device_id=(member, slab), device_id_type=MESH,
        )

    loads = [
        pltpu.make_async_copy(ref, raw.at[i], in_sem.at[i])
        for i, ref in enumerate((east_in, water_in, south_in))
    ] + [
        pltpu.make_async_copy(ref, raw_bed.at[i], in_sem.at[3 + i])
        for i, ref in enumerate((bed_in, rough_in))
    ]
    small = [
        pltpu.make_async_copy(ref, dst, in_sem.at[5 + i])
        for i, (ref, dst) in enumerate(
            ((gauges_in, gauges), (observed_in, observed), (ancestors_in, ancestors))
        )
    ]
    for copy in loads + small:
        copy.start()

    barrier = pltpu.get_barrier_semaphore()

    def greet(member, slab):
        pl.semaphore_signal(barrier, inc=1, device_id=(member, slab), device_id_type=MESH)

    for slab, there in ((up, has_up), (down, has_down)):

        @pl.when(there == 1)
        def _(slab=slab):
            greet(m, slab)
            greet(across, slab)

    @pl.loop(1, members)
    def _(i):
        greet(lax.rem(m + i, members), s)

    for copy in loads:
        copy.wait()

    def lay_out(r):
        from_row = (r // 8) * (8 * SUB) + lax.rem(r, 8)
        for i in range(3):
            for p in range(PARTS):
                a[3 * (r + RIM) + i, p] = raw[i, pl.ds(p * ROWS * SUB + from_row, SUB, stride=8)]
        bed[r + RIM, 0] = raw_bed[0, pl.ds(from_row, SUB, stride=8)]
        rough = raw_bed[1, pl.ds(from_row, SUB, stride=8)]
        bed[r + RIM, 1] = (gravity * time_step) * rough * rough

    @pl.loop(0, RIM)
    def _(r):
        lay_out(r)
        lay_out(ROWS - 1 - r)

    pl.semaphore_wait(barrier, members - 1 + 2 * (has_up + has_down))

    low, high = 3 * RIM, 3 * (RIM + ROWS)
    halos_down = [
        remote(bed.at[pl.ds(ROWS, RIM)], bed.at[pl.ds(0, RIM)], halo_send.at[0], halo_recv.at[0], across, down),
        remote(a.at[pl.ds(high - 5, 5)], a.at[pl.ds(low - 5, 5)], halo_send.at[2], halo_recv.at[2], m, down),
    ]
    halos_up = [
        remote(bed.at[pl.ds(RIM, RIM)], bed.at[pl.ds(RIM + ROWS, RIM)], halo_send.at[1], halo_recv.at[1], across, up),
        remote(a.at[pl.ds(low, 3)], a.at[pl.ds(high, 3)], halo_send.at[3], halo_recv.at[3], m, up),
        remote(a.at[pl.ds(low + 4, 1)], a.at[pl.ds(high + 4, 1)], halo_send.at[4], halo_recv.at[4], m, up),
    ]

    def toward(there, copies, act):
        @pl.when(there == 1)
        def _():
            for copy in copies:
                act(copy)

    toward(has_down, halos_down, lambda copy: copy.start())
    toward(has_up, halos_up, lambda copy: copy.start())

    def announce(t):
        @pl.when(s >= 2**t)
        def _():
            pl.semaphore_signal(here_sem.at[2 * t], inc=1, device_id=(m, s - 2**t), device_id_type=MESH)

        @pl.when(s + 2**t < slabs)
        def _():
            pl.semaphore_signal(here_sem.at[2 * t + 1], inc=1, device_id=(m, s + 2**t), device_id_type=MESH)

    def heard(t):
        @pl.when(s + 2**t < slabs)
        def _():
            pl.semaphore_wait(here_sem.at[2 * t], 1)

        @pl.when(s >= 2**t)
        def _():
            pl.semaphore_wait(here_sem.at[2 * t + 1], 1)

    announce(0)

    @pl.loop(RIM, ROWS - RIM)
    def _(r):
        lay_out(r)

    step_rows(a, bed, 1, ROWS - 2, 7, first, last_row, keep_in(b, RIM))
    step_rows(b, bed, 2, ROWS - 4, 4, first, last_row, keep_in(c, 0))

    heard(0)
    announce(1)

    def spread(to, f):
        return remote(c.at[3 * to + f], held[f].at[m], s1.at[f], r1.at[f], to, s)

    def batch(src, dst, count, send, recv):
        return remote(src.at[pl.ds(0, count)], dst.at[pl.ds(0, count)], send, recv, across, s)

    def spread_all(f):
        return batch(c, held[f], members - 1, s1.at[f], r1.at[f])

    for copy in small:
        copy.wait()

    cell = gauges[...] - first * (SUB * LANES)
    block = cell >> 7
    lane = cell & (LANES - 1)
    count = cell.shape[1]
    blocks = ROWS * SUB
    pick[...] = jnp.where(
        lax.broadcasted_iota(jnp.int32, (blocks, count), 0) == block, 1.0, 0.0
    ).astype(jnp.bfloat16)
    inside = jnp.logical_and(block >= 0, block < blocks)
    here = jnp.logical_and(
        lax.broadcasted_iota(jnp.int32, (LANES, count), 0) == lane, inside
    )

    heard(1)
    announce(2)
    heard(2)
    announce(3)
    toward(has_up, halos_down, lambda copy: copy.wait_recv())
    toward(has_down, halos_up, lambda copy: copy.wait_recv())

    step_rows(a, bed, -1, 2, 2, first, last_row, keep_in(b, RIM))
    step_rows(a, bed, ROWS - 1, 2, 2, first, last_row, keep_in(b, RIM))
    step_rows(b, bed, 0, 2, 2, first, last_row, keep_in(c, 0))
    step_rows(b, bed, ROWS - 2, 2, 2, first, last_row, keep_in(c, 0))

    def send_field(f):
        @pl.loop(1, members)
        def _(i):
            spread(lax.rem(m + i, members), f).start()

    send_field(0)

    rim_slots = [3 * ROWS - 5 + i for i in range(5)] + [0, 1, 2, 4]
    rims = [
        remote(c.at[rim_slots[i]], held_rim.at[m], sh.at[i // 5], rh.at[0], member, slab)
        for i, (member, slab) in enumerate(holder)
    ]
    toward(has_down, rims[:5], lambda copy: copy.start())
    toward(has_up, rims[5:], lambda copy: copy.start())

    send_field(1)
    send_field(2)
    heard(3)
    announce(4)

    water = jnp.concatenate(
        [jnp.concatenate([c[3 * r + WATER, p] for r in range(ROWS)], axis=0).T for p in range(PARTS)], axis=0
    )
    value = jnp.zeros((PARTS * LANES, count), jnp.float32)
    for _ in range(3):
        part = water.astype(jnp.bfloat16)
        value += jnp.dot(part, pick[...], preferred_element_type=jnp.float32)
        water = water - part.astype(jnp.float32)
    at_lane = lax.broadcasted_iota(jnp.int32, (1, LANES), 1)
    entry = jnp.zeros((1, LANES), jnp.float32)
    for p in range(PARTS):
        misfit = jnp.where(here, (value[p * LANES : (p + 1) * LANES] - observed[...]) ** 2, 0.0)
        total = jnp.sum(jnp.sum(misfit, axis=0, keepdims=True), axis=1, keepdims=True)
        entry = jnp.where(at_lane == PARTS * s + p, total, entry)
    z = s // 2
    z_lik[z] = entry

    def share(i):
        return remote(z_lik.at[z], z_lik.at[z], ls.at[0], lr.at[0], m, lax.rem(s + 2 * i, slabs))

    def share_all():
        heard(4)

        @pl.loop(1, slabs // 2)
        def _(i):
            share(i).start()

    for f in range(3):
        held[f][m] = c[3 * m + f]
    bed_copy = pltpu.make_async_copy(bed, bed_out, own_sem.at[6])
    bed_copy.start()

    def route(to, f):
        return remote(out.at[to, f], state_out.at[3 * (m + RIM) + f], s2.at[f], r2.at[f], to, s)

    def route_all(f):
        return batch(c, state_out, members - 1, s2.at[f], r2.at[f])

    def route_rim(to):
        return remote(out_rim.at[to], state_out.at[rim_slot], s2h.at[0], r2h.at[rim_at], to, s)

    def wanted(to, f):
        for k in range(PARTS):
            q = ancestors[PARTS * to + k]
            out[to, f, k] = held[f][q // PARTS, lax.rem(q, PARTS)]

    def wanted_rim(to):
        for k in range(PARTS):
            q = ancestors[PARTS * to + k]
            out_rim[to, k] = held_rim[q // PARTS, lax.rem(q, PARTS)]

    def mine(f):
        return pltpu.make_async_copy(out.at[m, f], state_out.at[3 * (m + RIM) + f], own_sem.at[f])

    def route_field(f):
        spread_all(f).wait_recv()

        @pl.loop(1, members)
        def _(i):
            to = lax.rem(m + i, members)
            wanted(to, f)
            route(to, f).start()

        wanted(m, f)
        mine(f).start()


    @pl.when(s >= slabs // 4)
    def _():
        share_all()

    route_field(0)

    route_field(1)

    route_field(2)

    rim_here = jnp.logical_or(
        jnp.logical_and(rim_at < 5, has_up == 1),
        jnp.logical_and(jnp.logical_and(rim_at >= 5, rim_at < HOLDERS), has_down == 1),
    )

    @pl.when(rim_here)
    def _():
        batch(c, held_rim, members, sh.at[0], rh.at[0]).wait_recv()

        @pl.loop(1, members)
        def _(i):
            to = lax.rem(m + i, members)
            wanted_rim(to)
            route_rim(to).start()

        wanted_rim(m)
        pltpu.make_async_copy(out_rim.at[m], state_out.at[rim_slot], own_sem.at[3]).start()

    @pl.when(s < slabs // 4)
    def _():
        share_all()

    share_batch = batch(z_lik, z_lik, slabs // 2 - 1, ls.at[0], lr.at[0])
    share_batch.wait_recv()
    entry = z_lik[0]
    for i in range(1, slabs // 2):
        entry = entry + z_lik[i]
    sums[...] = entry
    side = members * lax.rem(s, 2)
    twin = s + 1 - 2 * lax.rem(s, 2)

    def tell(to):
        return remote(sums, lik_out.at[side + m], ms.at[0], mr.at[0], to, s)

    def tell_twin(to):
        return remote(sums, lik_out.at[side + m], ms.at[0], mr.at[0], to, twin)

    @pl.loop(0, members)
    def _(i):
        tell_twin(lax.rem(m + i, members)).start()

    @pl.loop(1, members)
    def _(i):
        tell(lax.rem(m + i, members)).start()

    mine_lik = pltpu.make_async_copy(sums, lik_out.at[side + m], own_sem.at[5])
    mine_lik.start()

    toward(has_down, halos_down + [batch(c, held_rim, 5, sh.at[0], rh.at[0])], lambda copy: copy.wait_send())
    toward(has_up, halos_up + [batch(c, held_rim, 4, sh.at[1], rh.at[0])], lambda copy: copy.wait_send())

    tell_batch = batch(lik_out, lik_out, 2 * members - 1, ms.at[0], mr.at[0])
    share_batch.wait_send()
    tell_batch.wait_send()
    for f in range(3):
        spread_all(f).wait_send()
        route_all(f).wait_send()

    @pl.when(rim_here)
    def _():
        batch(c, held_rim, members - 1, s2h.at[0], rh.at[0]).wait_send()

    for f in range(3):
        route_all(f).wait_recv()
    tell_batch.wait_recv()

    for i, (member, _) in enumerate(holder):
        slot = 1 + i + 48 * (i // 5) + i // 8

        @pl.when(jnp.logical_and(m != member, (has_up if i < 5 else has_down) == 1))
        def _(i=i, slot=slot, member=member):
            remote(out_rim.at[0], state_out.at[slot], s2h.at[0], r2h.at[i], across, s).wait_recv()

    bed_copy.wait()
    for f in range(3):
        mine(f).wait()
    mine_lik.wait()

    @pl.when(rim_here)
    def _():
        pltpu.make_async_copy(out_rim.at[m], state_out.at[rim_slot], own_sem.at[3]).wait()


def finish_kernel(
    slabs, state_in, bed_in, lik_in, water_out, east_out, south_out, weight_out,
    a, b, bed, lik, done, in_sem, out_sem,
):
    m = lax.axis_index("member")
    s = lax.axis_index("space")
    first = s * ROWS
    last_row = slabs * ROWS - 1
    half = ROWS // 2
    cut = 3 * (half + 2 * RIM)
    loads = [
        pltpu.make_async_copy(bed_in, bed, in_sem.at[0]),
        pltpu.make_async_copy(state_in.at[pl.ds(0, cut)], a.at[pl.ds(0, cut)], in_sem.at[1]),
        pltpu.make_async_copy(state_in.at[pl.ds(cut, 3 * EXT - cut)], a.at[pl.ds(cut, 3 * EXT - cut)], in_sem.at[2]),
        pltpu.make_async_copy(lik_in, lik, in_sem.at[3]),
    ]
    for copy in loads[3:] + loads[:3]:
        copy.start()

    def store(row, p, field, value):
        start = p * ROWS * SUB + (row // 8) * (8 * SUB) + lax.rem(row, 8)
        done[field, pl.ds(start, SUB, stride=8)] = value

    copies = []

    def write(part):
        for p in range(PARTS):
            at = pl.ds((2 * p + part) * half * SUB, half * SUB)
            for i, ref in enumerate((east_out, water_out, south_out)):
                copy = pltpu.make_async_copy(done.at[i, at], ref.at[at], out_sem.at[part, p, i])
                copy.start()
                copies.append(copy)

    loads[3].wait()

    members = lik.shape[0] // 2
    rows = lik[0:members] + lik[members : 2 * members]
    own = lax.broadcasted_iota(jnp.int32, rows.shape, 0) == m
    lane = lax.broadcasted_iota(jnp.int32, rows.shape, 2)
    totals = []
    for p in range(PARTS):
        total = jnp.sum(jnp.where(lax.rem(lane, PARTS) == p, rows, 0.0), axis=2, keepdims=True)
        totals.append(-0.5 * jnp.broadcast_to(total, rows.shape))
    top = jnp.max(functools.reduce(jnp.maximum, totals))
    once = lane == 0
    mass = jnp.sum(jnp.where(once, sum(jnp.exp(total - top) for total in totals), 0.0))
    log_mass = jnp.log(jnp.broadcast_to(mass, rows.shape))
    for p in range(PARTS):
        weights = totals[p] - top - log_mass
        weight_out[p] = jnp.sum(jnp.where(jnp.logical_and(own, once), weights, 0.0))
    loads[0].wait()
    loads[1].wait()
    step_rows(a, bed, -1, half + 2, 5, first, last_row, keep_in(b, RIM))
    step_rows(b, bed, 0, half, 4, first, last_row, store)
    write(0)
    loads[2].wait()
    step_rows(a, bed, half + 1, half, 4, first, last_row, keep_in(b, RIM))
    step_rows(b, bed, half, half, 4, first, last_row, store)
    write(1)
    for copy in copies:
        copy.wait()


def to_blocks(x):
    lead = x.shape[:-2]
    n = len(lead)
    x = x.reshape(*lead, x.shape[-2] // 8, 8, SUB, LANES)
    x = x.transpose(*range(n), n, n + 2, n + 1, n + 3)
    return x.reshape(-1, LANES)


def from_blocks(x, parts, rows, width):
    x = x.reshape(parts, rows // 8, SUB, 8, LANES).transpose(0, 1, 3, 2, 4)
    return x.reshape(parts, rows, width)


def shards(members, slabs, depth, flow_x, flow_y, terrain, roughness, gauges, observed, ancestors):
    parts, rows, width = depth.shape
    f32 = jnp.float32
    hbm = pl.BlockSpec(memory_space=pl.ANY)
    smem = pl.BlockSpec(memory_space=pltpu.SMEM)
    row = (PARTS, SUB, LANES)
    dma = pltpu.SemaphoreType.DMA
    steps = slabs.bit_length() - 1
    count = gauges.shape[0]
    cells = parts * rows * SUB
    state, bed, lik = pl.pallas_call(
        functools.partial(exchange_kernel, members, slabs),
        out_shape=(
            jax.ShapeDtypeStruct((3 * EXT, *row), f32),
            jax.ShapeDtypeStruct((EXT, 2, SUB, LANES), f32),
            jax.ShapeDtypeStruct((2 * members, 1, LANES), f32),
        ),
        in_specs=[hbm] * 8,
        out_specs=(hbm, hbm, hbm),
        scratch_shapes=[
            pltpu.VMEM((3, cells, LANES), f32),
            pltpu.VMEM((2, rows * SUB, LANES), f32),
            pltpu.VMEM((3 * EXT, *row), f32),
            pltpu.VMEM((3 * EXT, *row), f32),
            pltpu.VMEM((3 * ROWS, *row), f32),
            pltpu.VMEM((EXT, 2, SUB, LANES), f32),
            pltpu.VMEM((members, *row), f32),
            pltpu.VMEM((members, *row), f32),
            pltpu.VMEM((members, *row), f32),
            pltpu.VMEM((members, *row), f32),
            pltpu.VMEM((members, 3, *row), f32),
            pltpu.VMEM((members, *row), f32),
            pltpu.VMEM((rows * SUB, count), jnp.bfloat16),
            pltpu.VMEM((slabs // 2, 1, LANES), f32),
            pltpu.VMEM((1, LANES), f32),
            pltpu.VMEM((1, count), jnp.int32),
            pltpu.VMEM((1, count), f32),
            pltpu.SMEM((members * PARTS,), jnp.int32),
            dma((8,)),
            dma((5,)), dma((5,)),
            dma((3,)), dma((3,)),
            dma((2,)), dma((1,)),
            dma((3,)), dma((3,)),
            dma((1,)), dma((HOLDERS,)),
            dma((1,)), dma((1,)),
            dma((1,)), dma((1,)),
            dma((7,)),
            pltpu.SemaphoreType.REGULAR((2 * steps,)),
        ],
        compiler_params=pltpu.CompilerParams(
            collective_id=0, has_side_effects=True, vmem_limit_bytes=VMEM_LIMIT
        ),
        name="exchange",
    )(
        to_blocks(depth), to_blocks(flow_x), to_blocks(flow_y), to_blocks(terrain), to_blocks(roughness),
        gauges.reshape(1, -1), observed.reshape(1, -1), ancestors,
    )
    water, east, south, weight = pl.pallas_call(
        functools.partial(finish_kernel, slabs),
        out_shape=(jax.ShapeDtypeStruct((cells, LANES), f32),) * 3
        + (jax.ShapeDtypeStruct((parts,), f32),),
        in_specs=[hbm] * 3,
        out_specs=(hbm, hbm, hbm, smem),
        scratch_shapes=[
            pltpu.VMEM((3 * EXT, *row), f32),
            pltpu.VMEM((3 * EXT, *row), f32),
            pltpu.VMEM((EXT, 2, SUB, LANES), f32),
            pltpu.VMEM((2 * members, 1, LANES), f32),
            pltpu.VMEM((3, cells, LANES), f32),
            dma((4,)), dma((2, PARTS, 3)),
        ],
        compiler_params=pltpu.CompilerParams(vmem_limit_bytes=VMEM_LIMIT),
        name="finish",
    )(state, bed, lik)
    back = functools.partial(from_blocks, parts=parts, rows=rows, width=width)
    return back(water), back(east), back(south), weight


def solution(mesh):
    placed = (P("member", "space", None),) * 3 + (P("space", None),) * 2 + (P(),) * 3
    return jax.shard_map(
        functools.partial(shards, mesh.shape["member"], mesh.shape["space"]),
        mesh=mesh,
        in_specs=placed,
        out_specs=(P("member", "space", None),) * 3 + (P("member"),),
        check_vma=False,
    )
```

```python
import functools

import jax
import jax.numpy as jnp
from jax import lax
from jax.experimental import pallas as pl
from jax.experimental.pallas import tpu as pltpu
from jax.sharding import PartitionSpec as P

MESH = pl.DeviceIdType.MESH
gravity = 9.81
time_step = 1.0
cell_size = 30.0
depth_floor = 0.1

EAST, WATER, SOUTH = 0, 1, 2
ROWS = 16
LANES = 128
PARTS = 2
SUB = 16
RIM = 2
EXT = ROWS + 2 * RIM
HOLDERS = 9
VMEM_LIMIT = 60 * 2**20


def next_column(x):
    y = pltpu.roll(x, LANES - 1, 1)
    lane = lax.broadcasted_iota(jnp.int32, x.shape, 1)
    return jnp.where(lane == LANES - 1, pltpu.roll(y, SUB - 1, 0), y)


def previous_column(x):
    y = pltpu.roll(x, 1, 1)
    lane = lax.broadcasted_iota(jnp.int32, x.shape, 1)
    return jnp.where(lane == 0, pltpu.roll(y, 1, 0), y)


def face(flow, eta_a, eta_b, bed_top, friction):
    hflow = jnp.maximum(jnp.maximum(eta_a, eta_b) - bed_top, depth_floor)
    push = flow - (gravity * time_step / cell_size) * hflow * (eta_b - eta_a)
    drag = 1.0 + friction * jnp.abs(flow) * jnp.exp2(lax.log2(hflow) * (-7.0 / 3.0))
    inverse = pl.reciprocal(drag, approx=True)
    inverse = inverse * (2.0 - drag * inverse)
    return push * inverse


def south_flow(src, bed, row, first, last_row):
    at = row + RIM
    bed_a, bed_b = bed[at, 0], bed[at + 1, 0]
    bed_top = jnp.maximum(bed_a, bed_b)
    friction = bed[at, 1]
    ok = jnp.logical_and(first + row >= 0, first + row < last_row)
    out = []
    for p in range(PARTS):
        eta_a = bed_a + src[3 * at + WATER, p]
        eta_b = bed_b + src[3 * (at + 1) + WATER, p]
        flow = face(src[3 * at + SOUTH, p], eta_a, eta_b, bed_top, friction)
        out.append(jnp.where(ok, flow, 0.0))
    return tuple(out)


def step_rows(src, bed, low, count, unroll, first, last_row, store):
    sub = lax.broadcasted_iota(jnp.int32, (SUB, LANES), 0)
    lane = lax.broadcasted_iota(jnp.int32, (SUB, LANES), 1)
    rim = jnp.logical_and(sub == SUB - 1, lane == LANES - 1)

    def one(i, north):
        row = low + i
        at = row + RIM
        south = south_flow(src, bed, row, first, last_row)
        bed_a = bed[at, 0]
        bed_top = jnp.maximum(bed_a, next_column(bed_a))
        friction = bed[at, 1]
        for p in range(PARTS):
            water = src[3 * at + WATER, p]
            eta = bed_a + water
            east = face(src[3 * at + EAST, p], eta, next_column(eta), bed_top, friction)
            east = jnp.where(rim, 0.0, east)
            west = previous_column(east)
            new = water + (time_step / cell_size) * (west - east + north[p] - south[p])
            store(row, p, EAST, east)
            store(row, p, WATER, new)
            store(row, p, SOUTH, south[p])
        return south

    def some(i, north):
        for k in range(unroll):
            north = one(i * unroll + k, north)
        return north

    north = south_flow(src, bed, low - 1, first, last_row)
    if count == unroll:
        some(0, north)
    else:
        lax.fori_loop(0, count // unroll, some, north)


def keep_in(dst, rim):
    def store(row, p, field, value):
        dst[3 * (row + rim) + field, p] = value

    return store


def exchange_kernel(
    members, slabs,
    water_in, east_in, south_in, bed_in, rough_in, gauges_in, observed_in, ancestors_in,
    state_out, bed_out, lik_out,
    raw, raw_bed, a, b, c, bed, held_a, held_b, held_c, held_rim, out, out_rim, pick, z_lik, sums,
    gauges, observed, ancestors, in_sem, halo_send, halo_recv, s1, r1, sh, rh, s2, r2, s2h, r2h, ls, lr, ms, mr, own_sem, here_sem,
):
    m = lax.axis_index("member")
    s = lax.axis_index("space")
    up = lax.rem(s + slabs - 1, slabs)
    down = lax.rem(s + 1, slabs)
    across = lax.rem(m + members // 2, members)
    first = s * ROWS
    last_row = slabs * ROWS - 1
    rim_at = m // 2 + 8 * lax.rem(m, 2)
    rim_slot = 1 + rim_at + 48 * (rim_at // 5) + rim_at // 8
    held = (held_a, held_b, held_c)
    has_up = (s + slabs - 1) // slabs
    has_down = (2 * slabs - 2 - s) // slabs
    holder = [(2 * i if i < 8 else 1, down if i < 5 else up) for i in range(HOLDERS)]

    def remote(src, dst, send, recv, member, slab):
        return pltpu.make_async_remote_copy(
            src_ref=src, dst_ref=dst, send_sem=send, recv_sem=recv,
            device_id=(member, slab), device_id_type=MESH,
        )

    loads = [
        pltpu.make_async_copy(ref, raw.at[i], in_sem.at[i])
        for i, ref in enumerate((east_in, water_in, south_in))
    ] + [
        pltpu.make_async_copy(ref, raw_bed.at[i], in_sem.at[3 + i])
        for i, ref in enumerate((bed_in, rough_in))
    ]
    small = [
        pltpu.make_async_copy(ref, dst, in_sem.at[5 + i])
        for i, (ref, dst) in enumerate(
            ((gauges_in, gauges), (observed_in, observed), (ancestors_in, ancestors))
        )
    ]
    for copy in loads + small:
        copy.start()

    barrier = pltpu.get_barrier_semaphore()

    def greet(member, slab):
        pl.semaphore_signal(barrier, inc=1, device_id=(member, slab), device_id_type=MESH)

    for slab, there in ((up, has_up), (down, has_down)):

        @pl.when(there == 1)
        def _(slab=slab):
            greet(m, slab)
            greet(across, slab)

    @pl.loop(1, members)
    def _(i):
        greet(lax.rem(m + i, members), s)

    for copy in loads:
        copy.wait()

    def lay_out(r):
        from_row = (r // 8) * (8 * SUB) + lax.rem(r, 8)
        for i in range(3):
            for p in range(PARTS):
                a[3 * (r + RIM) + i, p] = raw[i, pl.ds(p * ROWS * SUB + from_row, SUB, stride=8)]
        bed[r + RIM, 0] = raw_bed[0, pl.ds(from_row, SUB, stride=8)]
        rough = raw_bed[1, pl.ds(from_row, SUB, stride=8)]
        bed[r + RIM, 1] = (gravity * time_step) * rough * rough

    @pl.loop(0, RIM)
    def _(r):
        lay_out(r)
        lay_out(ROWS - 1 - r)

    pl.semaphore_wait(barrier, members - 1 + 2 * (has_up + has_down))

    low, high = 3 * RIM, 3 * (RIM + ROWS)
    halos_down = [
        remote(bed.at[pl.ds(ROWS, RIM)], bed.at[pl.ds(0, RIM)], halo_send.at[0], halo_recv.at[0], across, down),
        remote(a.at[pl.ds(high - 5, 5)], a.at[pl.ds(low - 5, 5)], halo_send.at[2], halo_recv.at[2], m, down),
    ]
    halos_up = [
        remote(bed.at[pl.ds(RIM, RIM)], bed.at[pl.ds(RIM + ROWS, RIM)], halo_send.at[1], halo_recv.at[1], across, up),
        remote(a.at[pl.ds(low, 3)], a.at[pl.ds(high, 3)], halo_send.at[3], halo_recv.at[3], m, up),
        remote(a.at[pl.ds(low + 4, 1)], a.at[pl.ds(high + 4, 1)], halo_send.at[4], halo_recv.at[4], m, up),
    ]

    def toward(there, copies, act):
        @pl.when(there == 1)
        def _():
            for copy in copies:
                act(copy)

    toward(has_down, halos_down, lambda copy: copy.start())
    toward(has_up, halos_up, lambda copy: copy.start())

    def announce(t):
        @pl.when(s >= 2**t)
        def _():
            pl.semaphore_signal(here_sem.at[2 * t], inc=1, device_id=(m, s - 2**t), device_id_type=MESH)

        @pl.when(s + 2**t < slabs)
        def _():
            pl.semaphore_signal(here_sem.at[2 * t + 1], inc=1, device_id=(m, s + 2**t), device_id_type=MESH)

    def heard(t):
        @pl.when(s + 2**t < slabs)
        def _():
            pl.semaphore_wait(here_sem.at[2 * t], 1)

        @pl.when(s >= 2**t)
        def _():
            pl.semaphore_wait(here_sem.at[2 * t + 1], 1)

    announce(0)

    @pl.loop(RIM, ROWS - RIM)
    def _(r):
        lay_out(r)

    step_rows(a, bed, 1, ROWS - 2, 7, first, last_row, keep_in(b, RIM))
    step_rows(b, bed, 2, ROWS - 4, 4, first, last_row, keep_in(c, 0))

    heard(0)
    announce(1)

    def spread(to, f):
        return remote(c.at[3 * to + f], held[f].at[m], s1.at[f], r1.at[f], to, s)

    def batch(src, dst, count, send, recv):
        return remote(src.at[pl.ds(0, count)], dst.at[pl.ds(0, count)], send, recv, across, s)

    def spread_all(f):
        return batch(c, held[f], members - 1, s1.at[f], r1.at[f])

    for copy in small:
        copy.wait()

    cell = gauges[...] - first * (SUB * LANES)
    block = cell >> 7
    lane = cell & (LANES - 1)
    count = cell.shape[1]
    blocks = ROWS * SUB
    pick[...] = jnp.where(
        lax.broadcasted_iota(jnp.int32, (blocks, count), 0) == block, 1.0, 0.0
    ).astype(jnp.bfloat16)
    inside = jnp.logical_and(block >= 0, block < blocks)
    here = jnp.logical_and(
        lax.broadcasted_iota(jnp.int32, (LANES, count), 0) == lane, inside
    )

    heard(1)
    announce(2)
    def third():
        heard(2)
        announce(3)

    @pl.when(s >= slabs // 4)
    def _():
        third()

    toward(has_up, halos_down, lambda copy: copy.wait_recv())
    toward(has_down, halos_up, lambda copy: copy.wait_recv())

    step_rows(a, bed, -1, 2, 2, first, last_row, keep_in(b, RIM))
    step_rows(a, bed, ROWS - 1, 2, 2, first, last_row, keep_in(b, RIM))
    step_rows(b, bed, 0, 2, 2, first, last_row, keep_in(c, 0))
    step_rows(b, bed, ROWS - 2, 2, 2, first, last_row, keep_in(c, 0))

    def send_field(f):
        @pl.loop(1, members)
        def _(i):
            spread(lax.rem(m + i, members), f).start()

    def fourth():
        heard(3)
        announce(4)

    @pl.when(s >= slabs // 2)
    def _():
        fourth()

    send_field(0)

    rim_slots = [3 * ROWS - 5 + i for i in range(5)] + [0, 1, 2, 4]
    rims = [
        remote(c.at[rim_slots[i]], held_rim.at[m], sh.at[i // 5], rh.at[0], member, slab)
        for i, (member, slab) in enumerate(holder)
    ]
    toward(has_down, rims[:5], lambda copy: copy.start())
    toward(has_up, rims[5:], lambda copy: copy.start())

    send_field(1)
    send_field(2)
    @pl.when(s < slabs // 4)
    def _():
        third()

    @pl.when(s < slabs // 2)
    def _():
        fourth()


    water = jnp.concatenate(
        [jnp.concatenate([c[3 * r + WATER, p] for r in range(ROWS)], axis=0).T for p in range(PARTS)], axis=0
    )
    value = jnp.zeros((PARTS * LANES, count), jnp.float32)
    for _ in range(3):
        part = water.astype(jnp.bfloat16)
        value += jnp.dot(part, pick[...], preferred_element_type=jnp.float32)
        water = water - part.astype(jnp.float32)
    at_lane = lax.broadcasted_iota(jnp.int32, (1, LANES), 1)
    entry = jnp.zeros((1, LANES), jnp.float32)
    for p in range(PARTS):
        misfit = jnp.where(here, (value[p * LANES : (p + 1) * LANES] - observed[...]) ** 2, 0.0)
        total = jnp.sum(jnp.sum(misfit, axis=0, keepdims=True), axis=1, keepdims=True)
        entry = jnp.where(at_lane == PARTS * s + p, total, entry)
    z = s // 2
    z_lik[z] = entry

    def share(i):
        return remote(z_lik.at[z], z_lik.at[z], ls.at[0], lr.at[0], m, lax.rem(s + 2 * i, slabs))

    def share_all():
        heard(4)

        @pl.loop(1, slabs // 2)
        def _(i):
            share(i).start()

    for f in range(3):
        held[f][m] = c[3 * m + f]
    bed_copy = pltpu.make_async_copy(bed, bed_out, own_sem.at[6])
    bed_copy.start()

    def route(to, f):
        return remote(out.at[to, f], state_out.at[3 * (m + RIM) + f], s2.at[f], r2.at[f], to, s)

    def route_all(f):
        return batch(c, state_out, members - 1, s2.at[f], r2.at[f])

    def route_rim(to):
        return remote(out_rim.at[to], state_out.at[rim_slot], s2h.at[0], r2h.at[rim_at], to, s)

    def wanted(to, f):
        for k in range(PARTS):
            q = ancestors[PARTS * to + k]
            out[to, f, k] = held[f][q // PARTS, lax.rem(q, PARTS)]

    def wanted_rim(to):
        for k in range(PARTS):
            q = ancestors[PARTS * to + k]
            out_rim[to, k] = held_rim[q // PARTS, lax.rem(q, PARTS)]

    def mine(f):
        return pltpu.make_async_copy(out.at[m, f], state_out.at[3 * (m + RIM) + f], own_sem.at[f])

    def route_field(f):
        spread_all(f).wait_recv()

        @pl.loop(1, members)
        def _(i):
            to = lax.rem(m + i, members)
            wanted(to, f)
            route(to, f).start()

        wanted(m, f)
        mine(f).start()


    @pl.when(s >= slabs // 4)
    def _():
        share_all()

    route_field(0)

    route_field(1)

    @pl.when(s < slabs // 4)
    def _():
        share_all()

    route_field(2)

    rim_here = jnp.logical_or(
        jnp.logical_and(rim_at < 5, has_up == 1),
        jnp.logical_and(jnp.logical_and(rim_at >= 5, rim_at < HOLDERS), has_down == 1),
    )

    @pl.when(rim_here)
    def _():
        batch(c, held_rim, members, sh.at[0], rh.at[0]).wait_recv()

        @pl.loop(1, members)
        def _(i):
            to = lax.rem(m + i, members)
            wanted_rim(to)
            route_rim(to).start()

        wanted_rim(m)
        pltpu.make_async_copy(out_rim.at[m], state_out.at[rim_slot], own_sem.at[3]).start()

    share_batch = batch(z_lik, z_lik, slabs // 2 - 1, ls.at[0], lr.at[0])
    share_batch.wait_recv()
    entry = z_lik[0]
    for i in range(1, slabs // 2):
        entry = entry + z_lik[i]
    sums[...] = entry
    side = members * lax.rem(s, 2)
    twin = s + 1 - 2 * lax.rem(s, 2)

    def tell(to):
        return remote(sums, lik_out.at[side + m], ms.at[0], mr.at[0], to, s)

    def tell_twin(to):
        return remote(sums, lik_out.at[side + m], ms.at[0], mr.at[0], to, twin)

    @pl.loop(0, members)
    def _(i):
        tell_twin(lax.rem(m + i, members)).start()

    @pl.loop(1, members)
    def _(i):
        tell(lax.rem(m + i, members)).start()

    mine_lik = pltpu.make_async_copy(sums, lik_out.at[side + m], own_sem.at[5])
    mine_lik.start()

    toward(has_down, halos_down + [batch(c, held_rim, 5, sh.at[0], rh.at[0])], lambda copy: copy.wait_send())
    toward(has_up, halos_up + [batch(c, held_rim, 4, sh.at[1], rh.at[0])], lambda copy: copy.wait_send())

    tell_batch = batch(lik_out, lik_out, 2 * members - 1, ms.at[0], mr.at[0])
    share_batch.wait_send()
    tell_batch.wait_send()
    for f in range(3):
        spread_all(f).wait_send()
        route_all(f).wait_send()

    @pl.when(rim_here)
    def _():
        batch(c, held_rim, members - 1, s2h.at[0], rh.at[0]).wait_send()

    for f in range(3):
        route_all(f).wait_recv()
    tell_batch.wait_recv()

    for i, (member, _) in enumerate(holder):
        slot = 1 + i + 48 * (i // 5) + i // 8

        @pl.when(jnp.logical_and(m != member, (has_up if i < 5 else has_down) == 1))
        def _(i=i, slot=slot, member=member):
            remote(out_rim.at[0], state_out.at[slot], s2h.at[0], r2h.at[i], across, s).wait_recv()

    bed_copy.wait()
    for f in range(3):
        mine(f).wait()
    mine_lik.wait()

    @pl.when(rim_here)
    def _():
        pltpu.make_async_copy(out_rim.at[m], state_out.at[rim_slot], own_sem.at[3]).wait()


def finish_kernel(
    slabs, state_in, bed_in, lik_in, water_out, east_out, south_out, weight_out,
    a, b, bed, lik, done, weight, in_sem, out_sem,
):
    m = lax.axis_index("member")
    s = lax.axis_index("space")
    first = s * ROWS
    last_row = slabs * ROWS - 1
    half = ROWS // 2
    cut = 3 * (half + 2 * RIM)
    loads = [
        pltpu.make_async_copy(bed_in, bed, in_sem.at[0]),
        pltpu.make_async_copy(state_in.at[pl.ds(0, cut)], a.at[pl.ds(0, cut)], in_sem.at[1]),
        pltpu.make_async_copy(state_in.at[pl.ds(cut, 3 * EXT - cut)], a.at[pl.ds(cut, 3 * EXT - cut)], in_sem.at[2]),
        pltpu.make_async_copy(lik_in, lik, in_sem.at[3]),
    ]
    for copy in loads[3:] + loads[:3]:
        copy.start()

    def store(row, p, field, value):
        start = p * ROWS * SUB + (row // 8) * (8 * SUB) + lax.rem(row, 8)
        done[field, pl.ds(start, SUB, stride=8)] = value

    copies = []

    def write(part):
        for p in range(PARTS):
            at = pl.ds((2 * p + part) * half * SUB, half * SUB)
            for i, ref in enumerate((east_out, water_out, south_out)):
                copy = pltpu.make_async_copy(done.at[i, at], ref.at[at], out_sem.at[part, p, i])
                copy.start()
                copies.append(copy)

    loads[3].wait()

    members = lik.shape[0] // 2
    rows = lik[0:members] + lik[members : 2 * members]
    own = lax.broadcasted_iota(jnp.int32, rows.shape, 0) == m
    lane = lax.broadcasted_iota(jnp.int32, rows.shape, 2)
    totals = []
    for p in range(PARTS):
        total = jnp.sum(jnp.where(lax.rem(lane, PARTS) == p, rows, 0.0), axis=2, keepdims=True)
        totals.append(-0.5 * jnp.broadcast_to(total, rows.shape))
    top = jnp.max(functools.reduce(jnp.maximum, totals))
    once = lane == 0
    mass = jnp.sum(jnp.where(once, sum(jnp.exp(total - top) for total in totals), 0.0))
    log_mass = jnp.log(jnp.broadcast_to(mass, rows.shape))
    for p in range(PARTS):
        weights = totals[p] - top - log_mass
        weight[p] = jnp.sum(jnp.where(jnp.logical_and(own, once), weights, 0.0))
    copies.append(pltpu.make_async_copy(weight, weight_out, in_sem.at[4]))
    copies[0].start()
    loads[0].wait()
    loads[1].wait()
    step_rows(a, bed, -1, half + 2, 5, first, last_row, keep_in(b, RIM))
    step_rows(b, bed, 0, half, 4, first, last_row, store)
    write(0)
    loads[2].wait()
    step_rows(a, bed, half + 1, half, 4, first, last_row, keep_in(b, RIM))
    step_rows(b, bed, half, half, 4, first, last_row, store)
    write(1)
    for copy in copies:
        copy.wait()


def to_blocks(x):
    lead = x.shape[:-2]
    n = len(lead)
    x = x.reshape(*lead, x.shape[-2] // 8, 8, SUB, LANES)
    x = x.transpose(*range(n), n, n + 2, n + 1, n + 3)
    return x.reshape(-1, LANES)


def from_blocks(x, parts, rows, width):
    x = x.reshape(parts, rows // 8, SUB, 8, LANES).transpose(0, 1, 3, 2, 4)
    return x.reshape(parts, rows, width)


def shards(members, slabs, depth, flow_x, flow_y, terrain, roughness, gauges, observed, ancestors):
    parts, rows, width = depth.shape
    f32 = jnp.float32
    hbm = pl.BlockSpec(memory_space=pl.ANY)
    row = (PARTS, SUB, LANES)
    dma = pltpu.SemaphoreType.DMA
    steps = slabs.bit_length() - 1
    count = gauges.shape[0]
    cells = parts * rows * SUB
    state, bed, lik = pl.pallas_call(
        functools.partial(exchange_kernel, members, slabs),
        out_shape=(
            jax.ShapeDtypeStruct((3 * EXT, *row), f32),
            jax.ShapeDtypeStruct((EXT, 2, SUB, LANES), f32),
            jax.ShapeDtypeStruct((2 * members, 1, LANES), f32),
        ),
        in_specs=[hbm] * 8,
        out_specs=(hbm, hbm, hbm),
        scratch_shapes=[
            pltpu.VMEM((3, cells, LANES), f32),
            pltpu.VMEM((2, rows * SUB, LANES), f32),
            pltpu.VMEM((3 * EXT, *row), f32),
            pltpu.VMEM((3 * EXT, *row), f32),
            pltpu.VMEM((3 * ROWS, *row), f32),
            pltpu.VMEM((EXT, 2, SUB, LANES), f32),
            pltpu.VMEM((members, *row), f32),
            pltpu.VMEM((members, *row), f32),
            pltpu.VMEM((members, *row), f32),
            pltpu.VMEM((members, *row), f32),
            pltpu.VMEM((members, 3, *row), f32),
            pltpu.VMEM((members, *row), f32),
            pltpu.VMEM((rows * SUB, count), jnp.bfloat16),
            pltpu.VMEM((slabs // 2, 1, LANES), f32),
            pltpu.VMEM((1, LANES), f32),
            pltpu.VMEM((1, count), jnp.int32),
            pltpu.VMEM((1, count), f32),
            pltpu.SMEM((members * PARTS,), jnp.int32),
            dma((8,)),
            dma((5,)), dma((5,)),
            dma((3,)), dma((3,)),
            dma((2,)), dma((1,)),
            dma((3,)), dma((3,)),
            dma((1,)), dma((HOLDERS,)),
            dma((1,)), dma((1,)),
            dma((1,)), dma((1,)),
            dma((7,)),
            pltpu.SemaphoreType.REGULAR((2 * steps,)),
        ],
        compiler_params=pltpu.CompilerParams(
            collective_id=0, has_side_effects=True, vmem_limit_bytes=VMEM_LIMIT
        ),
        name="exchange",
    )(
        to_blocks(depth), to_blocks(flow_x), to_blocks(flow_y), to_blocks(terrain), to_blocks(roughness),
        gauges.reshape(1, -1), observed.reshape(1, -1), ancestors,
    )
    water, east, south, weight = pl.pallas_call(
        functools.partial(finish_kernel, slabs),
        out_shape=(jax.ShapeDtypeStruct((cells, LANES), f32),) * 3
        + (jax.ShapeDtypeStruct((parts,), f32),),
        in_specs=[hbm] * 3,
        out_specs=(hbm, hbm, hbm, hbm),
        scratch_shapes=[
            pltpu.VMEM((3 * EXT, *row), f32),
            pltpu.VMEM((3 * EXT, *row), f32),
            pltpu.VMEM((EXT, 2, SUB, LANES), f32),
            pltpu.VMEM((2 * members, 1, LANES), f32),
            pltpu.VMEM((3, cells, LANES), f32),
            pltpu.SMEM((parts,), f32),
            dma((5,)), dma((2, PARTS, 3)),
        ],
        compiler_params=pltpu.CompilerParams(vmem_limit_bytes=VMEM_LIMIT),
        name="finish",
    )(state, bed, lik)
    back = functools.partial(from_blocks, parts=parts, rows=rows, width=width)
    return back(water), back(east), back(south), weight


def solution(mesh):
    placed = (P("member", "space", None),) * 3 + (P("space", None),) * 2 + (P(),) * 3
    return jax.shard_map(
        functools.partial(shards, mesh.shape["member"], mesh.shape["space"]),
        mesh=mesh,
        in_specs=placed,
        out_specs=(P("member", "space", None),) * 3 + (P("member"),),
        check_vma=False,
    )
```

```python
import functools

import jax
import jax.numpy as jnp
from jax import lax
from jax.experimental import pallas as pl
from jax.experimental.pallas import tpu as pltpu
from jax.sharding import PartitionSpec as P

MESH = pl.DeviceIdType.MESH
gravity = 9.81
time_step = 1.0
cell_size = 30.0
depth_floor = 0.1

EAST, WATER, SOUTH = 0, 1, 2
ROWS = 16
LANES = 128
PARTS = 2
SUB = 16
RIM = 2
EXT = ROWS + 2 * RIM
HOLDERS = 9
VMEM_LIMIT = 60 * 2**20


def next_column(x):
    y = pltpu.roll(x, LANES - 1, 1)
    lane = lax.broadcasted_iota(jnp.int32, x.shape, 1)
    return jnp.where(lane == LANES - 1, pltpu.roll(y, SUB - 1, 0), y)


def previous_column(x):
    y = pltpu.roll(x, 1, 1)
    lane = lax.broadcasted_iota(jnp.int32, x.shape, 1)
    return jnp.where(lane == 0, pltpu.roll(y, 1, 0), y)


def face(flow, eta_a, eta_b, bed_top, friction):
    hflow = jnp.maximum(jnp.maximum(eta_a, eta_b) - bed_top, depth_floor)
    push = flow - (gravity * time_step / cell_size) * hflow * (eta_b - eta_a)
    drag = 1.0 + friction * jnp.abs(flow) * jnp.exp2(lax.log2(hflow) * (-7.0 / 3.0))
    inverse = pl.reciprocal(drag, approx=True)
    inverse = inverse * (2.0 - drag * inverse)
    return push * inverse


def south_flow(src, bed, row, first, last_row):
    at = row + RIM
    bed_a, bed_b = bed[at, 0], bed[at + 1, 0]
    bed_top = jnp.maximum(bed_a, bed_b)
    friction = bed[at, 1]
    ok = jnp.logical_and(first + row >= 0, first + row < last_row)
    out = []
    for p in range(PARTS):
        eta_a = bed_a + src[3 * at + WATER, p]
        eta_b = bed_b + src[3 * (at + 1) + WATER, p]
        flow = face(src[3 * at + SOUTH, p], eta_a, eta_b, bed_top, friction)
        out.append(jnp.where(ok, flow, 0.0))
    return tuple(out)


def step_rows(src, bed, low, count, unroll, first, last_row, store):
    sub = lax.broadcasted_iota(jnp.int32, (SUB, LANES), 0)
    lane = lax.broadcasted_iota(jnp.int32, (SUB, LANES), 1)
    rim = jnp.logical_and(sub == SUB - 1, lane == LANES - 1)

    def one(i, north):
        row = low + i
        at = row + RIM
        south = south_flow(src, bed, row, first, last_row)
        bed_a = bed[at, 0]
        bed_top = jnp.maximum(bed_a, next_column(bed_a))
        friction = bed[at, 1]
        for p in range(PARTS):
            water = src[3 * at + WATER, p]
            eta = bed_a + water
            east = face(src[3 * at + EAST, p], eta, next_column(eta), bed_top, friction)
            east = jnp.where(rim, 0.0, east)
            west = previous_column(east)
            new = water + (time_step / cell_size) * (west - east + north[p] - south[p])
            store(row, p, EAST, east)
            store(row, p, WATER, new)
            store(row, p, SOUTH, south[p])
        return south

    def some(i, north):
        for k in range(unroll):
            north = one(i * unroll + k, north)
        return north

    north = south_flow(src, bed, low - 1, first, last_row)
    if count == unroll:
        some(0, north)
    else:
        lax.fori_loop(0, count // unroll, some, north)


def keep_in(dst, rim):
    def store(row, p, field, value):
        dst[3 * (row + rim) + field, p] = value

    return store


def exchange_kernel(
    members, slabs,
    water_in, east_in, south_in, bed_in, rough_in, gauges_in, observed_in, ancestors_in,
    state_out, bed_out, lik_out,
    raw, raw_bed, a, b, c, bed, held_a, held_b, held_c, held_rim, out, out_rim, pick, z_lik, sums,
    gauges, observed, ancestors, in_sem, halo_send, halo_recv, s1, r1, sh, rh, s2, r2, s2h, r2h, ls, lr, ms, mr, own_sem, here_sem,
):
    m = lax.axis_index("member")
    s = lax.axis_index("space")
    up = lax.rem(s + slabs - 1, slabs)
    down = lax.rem(s + 1, slabs)
    across = lax.rem(m + members // 2, members)
    first = s * ROWS
    last_row = slabs * ROWS - 1
    rim_at = m // 2 + 8 * lax.rem(m, 2)
    rim_slot = 1 + rim_at + 48 * (rim_at // 5) + rim_at // 8
    held = (held_a, held_b, held_c)
    has_up = (s + slabs - 1) // slabs
    has_down = (2 * slabs - 2 - s) // slabs
    holder = [(2 * i if i < 8 else 1, down if i < 5 else up) for i in range(HOLDERS)]

    def remote(src, dst, send, recv, member, slab):
        return pltpu.make_async_remote_copy(
            src_ref=src, dst_ref=dst, send_sem=send, recv_sem=recv,
            device_id=(member, slab), device_id_type=MESH,
        )

    loads = [
        pltpu.make_async_copy(ref, raw.at[i], in_sem.at[i])
        for i, ref in enumerate((east_in, water_in, south_in))
    ] + [
        pltpu.make_async_copy(ref, raw_bed.at[i], in_sem.at[3 + i])
        for i, ref in enumerate((bed_in, rough_in))
    ]
    small = [
        pltpu.make_async_copy(ref, dst, in_sem.at[5 + i])
        for i, (ref, dst) in enumerate(
            ((gauges_in, gauges), (observed_in, observed), (ancestors_in, ancestors))
        )
    ]
    for copy in loads + small:
        copy.start()

    barrier = pltpu.get_barrier_semaphore()

    def greet(member, slab):
        pl.semaphore_signal(barrier, inc=1, device_id=(member, slab), device_id_type=MESH)

    for slab, there in ((up, has_up), (down, has_down)):

        @pl.when(there == 1)
        def _(slab=slab):
            greet(m, slab)
            greet(across, slab)

    @pl.when(s >= 2)
    def _():
        greet(m, s - 2)

    @pl.when(s + 2 < slabs)
    def _():
        greet(m, s + 2)

    @pl.loop(1, members)
    def _(i):
        greet(lax.rem(m + i, members), s)

    for copy in loads:
        copy.wait()

    def lay_out(r):
        from_row = (r // 8) * (8 * SUB) + lax.rem(r, 8)
        for i in range(3):
            for p in range(PARTS):
                a[3 * (r + RIM) + i, p] = raw[i, pl.ds(p * ROWS * SUB + from_row, SUB, stride=8)]
        bed[r + RIM, 0] = raw_bed[0, pl.ds(from_row, SUB, stride=8)]
        rough = raw_bed[1, pl.ds(from_row, SUB, stride=8)]
        bed[r + RIM, 1] = (gravity * time_step) * rough * rough

    @pl.loop(0, RIM)
    def _(r):
        lay_out(r)
        lay_out(ROWS - 1 - r)

    two_away = (s + slabs - 2) // slabs + (2 * slabs - 3 - s) // slabs
    pl.semaphore_wait(barrier, members - 1 + 2 * (has_up + has_down) + two_away)

    low, high = 3 * RIM, 3 * (RIM + ROWS)
    halos_down = [
        remote(bed.at[pl.ds(ROWS, RIM)], bed.at[pl.ds(0, RIM)], halo_send.at[0], halo_recv.at[0], across, down),
        remote(a.at[pl.ds(high - 5, 5)], a.at[pl.ds(low - 5, 5)], halo_send.at[2], halo_recv.at[2], m, down),
    ]
    halos_up = [
        remote(bed.at[pl.ds(RIM, RIM)], bed.at[pl.ds(RIM + ROWS, RIM)], halo_send.at[1], halo_recv.at[1], across, up),
        remote(a.at[pl.ds(low, 3)], a.at[pl.ds(high, 3)], halo_send.at[3], halo_recv.at[3], m, up),
        remote(a.at[pl.ds(low + 4, 1)], a.at[pl.ds(high + 4, 1)], halo_send.at[4], halo_recv.at[4], m, up),
    ]

    def toward(there, copies, act):
        @pl.when(there == 1)
        def _():
            for copy in copies:
                act(copy)

    toward(has_down, halos_down, lambda copy: copy.start())
    toward(has_up, halos_up, lambda copy: copy.start())

    def announce(t):
        @pl.when(s >= 2**t)
        def _():
            pl.semaphore_signal(here_sem.at[2 * t], inc=1, device_id=(m, s - 2**t), device_id_type=MESH)

        @pl.when(s + 2**t < slabs)
        def _():
            pl.semaphore_signal(here_sem.at[2 * t + 1], inc=1, device_id=(m, s + 2**t), device_id_type=MESH)

    def heard(t):
        @pl.when(s + 2**t < slabs)
        def _():
            pl.semaphore_wait(here_sem.at[2 * t], 1)

        @pl.when(s >= 2**t)
        def _():
            pl.semaphore_wait(here_sem.at[2 * t + 1], 1)

    announce(1)

    @pl.loop(RIM, ROWS - RIM)
    def _(r):
        lay_out(r)

    step_rows(a, bed, 1, ROWS - 2, 7, first, last_row, keep_in(b, RIM))
    step_rows(b, bed, 2, ROWS - 4, 4, first, last_row, keep_in(c, 0))

    heard(1)
    announce(2)

    def spread(to, f):
        return remote(c.at[3 * to + f], held[f].at[m], s1.at[f], r1.at[f], to, s)

    def batch(src, dst, count, send, recv):
        return remote(src.at[pl.ds(0, count)], dst.at[pl.ds(0, count)], send, recv, across, s)

    def spread_all(f):
        return batch(c, held[f], members - 1, s1.at[f], r1.at[f])

    for copy in small:
        copy.wait()

    cell = gauges[...] - first * (SUB * LANES)
    block = cell >> 7
    lane = cell & (LANES - 1)
    count = cell.shape[1]
    blocks = ROWS * SUB
    pick[...] = jnp.where(
        lax.broadcasted_iota(jnp.int32, (blocks, count), 0) == block, 1.0, 0.0
    ).astype(jnp.bfloat16)
    inside = jnp.logical_and(block >= 0, block < blocks)
    here = jnp.logical_and(
        lax.broadcasted_iota(jnp.int32, (LANES, count), 0) == lane, inside
    )

    def third():
        heard(2)
        announce(3)

    @pl.when(s >= slabs // 4)
    def _():
        third()

    toward(has_up, halos_down, lambda copy: copy.wait_recv())
    toward(has_down, halos_up, lambda copy: copy.wait_recv())

    step_rows(a, bed, -1, 2, 2, first, last_row, keep_in(b, RIM))
    step_rows(a, bed, ROWS - 1, 2, 2, first, last_row, keep_in(b, RIM))
    step_rows(b, bed, 0, 2, 2, first, last_row, keep_in(c, 0))
    step_rows(b, bed, ROWS - 2, 2, 2, first, last_row, keep_in(c, 0))

    def send_field(f):
        @pl.loop(1, members)
        def _(i):
            spread(lax.rem(m + i, members), f).start()

    def fourth():
        heard(3)
        announce(4)

    @pl.when(s >= slabs // 2)
    def _():
        fourth()

    send_field(0)

    rim_slots = [3 * ROWS - 5 + i for i in range(5)] + [0, 1, 2, 4]
    rims = [
        remote(c.at[rim_slots[i]], held_rim.at[m], sh.at[i // 5], rh.at[0], member, slab)
        for i, (member, slab) in enumerate(holder)
    ]
    toward(has_down, rims[:5], lambda copy: copy.start())
    toward(has_up, rims[5:], lambda copy: copy.start())

    send_field(1)
    send_field(2)
    @pl.when(s < slabs // 4)
    def _():
        third()

    @pl.when(s < slabs // 2)
    def _():
        fourth()


    water = jnp.concatenate(
        [jnp.concatenate([c[3 * r + WATER, p] for r in range(ROWS)], axis=0).T for p in range(PARTS)], axis=0
    )
    value = jnp.zeros((PARTS * LANES, count), jnp.float32)
    for _ in range(3):
        part = water.astype(jnp.bfloat16)
        value += jnp.dot(part, pick[...], preferred_element_type=jnp.float32)
        water = water - part.astype(jnp.float32)
    at_lane = lax.broadcasted_iota(jnp.int32, (1, LANES), 1)
    entry = jnp.zeros((1, LANES), jnp.float32)
    for p in range(PARTS):
        misfit = jnp.where(here, (value[p * LANES : (p + 1) * LANES] - observed[...]) ** 2, 0.0)
        total = jnp.sum(jnp.sum(misfit, axis=0, keepdims=True), axis=1, keepdims=True)
        entry = jnp.where(at_lane == PARTS * s + p, total, entry)
    z = s // 2
    z_lik[z] = entry

    def share(i):
        return remote(z_lik.at[z], z_lik.at[z], ls.at[0], lr.at[0], m, lax.rem(s + 2 * i, slabs))

    def share_all():
        heard(4)

        @pl.loop(1, slabs // 2)
        def _(i):
            share(i).start()

    for f in range(3):
        held[f][m] = c[3 * m + f]
    bed_copy = pltpu.make_async_copy(bed, bed_out, own_sem.at[6])
    bed_copy.start()

    def route(to, f):
        return remote(out.at[to, f], state_out.at[3 * (m + RIM) + f], s2.at[f], r2.at[f], to, s)

    def route_all(f):
        return batch(c, state_out, members - 1, s2.at[f], r2.at[f])

    def route_rim(to):
        return remote(out_rim.at[to], state_out.at[rim_slot], s2h.at[0], r2h.at[rim_at], to, s)

    def wanted(to, f):
        for k in range(PARTS):
            q = ancestors[PARTS * to + k]
            out[to, f, k] = held[f][q // PARTS, lax.rem(q, PARTS)]

    def wanted_rim(to):
        for k in range(PARTS):
            q = ancestors[PARTS * to + k]
            out_rim[to, k] = held_rim[q // PARTS, lax.rem(q, PARTS)]

    def mine(f):
        return pltpu.make_async_copy(out.at[m, f], state_out.at[3 * (m + RIM) + f], own_sem.at[f])

    def route_field(f):
        spread_all(f).wait_recv()

        @pl.loop(1, members)
        def _(i):
            to = lax.rem(m + i, members)
            wanted(to, f)
            route(to, f).start()

        wanted(m, f)
        mine(f).start()


    @pl.when(s >= slabs // 4)
    def _():
        share_all()

    route_field(0)

    route_field(1)

    @pl.when(s < slabs // 4)
    def _():
        share_all()

    route_field(2)

    rim_here = jnp.logical_or(
        jnp.logical_and(rim_at < 5, has_up == 1),
        jnp.logical_and(jnp.logical_and(rim_at >= 5, rim_at < HOLDERS), has_down == 1),
    )

    @pl.when(rim_here)
    def _():
        batch(c, held_rim, members, sh.at[0], rh.at[0]).wait_recv()

        @pl.loop(1, members)
        def _(i):
            to = lax.rem(m + i, members)
            wanted_rim(to)
            route_rim(to).start()

        wanted_rim(m)
        pltpu.make_async_copy(out_rim.at[m], state_out.at[rim_slot], own_sem.at[3]).start()

    share_batch = batch(z_lik, z_lik, slabs // 2 - 1, ls.at[0], lr.at[0])
    share_batch.wait_recv()
    entry = z_lik[0]
    for i in range(1, slabs // 2):
        entry = entry + z_lik[i]
    sums[...] = entry
    side = members * lax.rem(s, 2)
    twin = s + 1 - 2 * lax.rem(s, 2)

    def tell(to):
        return remote(sums, lik_out.at[side + m], ms.at[0], mr.at[0], to, s)

    def tell_twin(to):
        return remote(sums, lik_out.at[side + m], ms.at[0], mr.at[0], to, twin)

    @pl.loop(0, members)
    def _(i):
        tell_twin(lax.rem(m + i, members)).start()

    @pl.loop(1, members)
    def _(i):
        tell(lax.rem(m + i, members)).start()

    mine_lik = pltpu.make_async_copy(sums, lik_out.at[side + m], own_sem.at[5])
    mine_lik.start()

    toward(has_down, halos_down + [batch(c, held_rim, 5, sh.at[0], rh.at[0])], lambda copy: copy.wait_send())
    toward(has_up, halos_up + [batch(c, held_rim, 4, sh.at[1], rh.at[0])], lambda copy: copy.wait_send())

    tell_batch = batch(lik_out, lik_out, 2 * members - 1, ms.at[0], mr.at[0])
    share_batch.wait_send()
    tell_batch.wait_send()
    for f in range(3):
        spread_all(f).wait_send()
        route_all(f).wait_send()

    @pl.when(rim_here)
    def _():
        batch(c, held_rim, members - 1, s2h.at[0], rh.at[0]).wait_send()

    for f in range(3):
        route_all(f).wait_recv()
    tell_batch.wait_recv()

    for i, (member, _) in enumerate(holder):
        slot = 1 + i + 48 * (i // 5) + i // 8

        @pl.when(jnp.logical_and(m != member, (has_up if i < 5 else has_down) == 1))
        def _(i=i, slot=slot, member=member):
            remote(out_rim.at[0], state_out.at[slot], s2h.at[0], r2h.at[i], across, s).wait_recv()

    bed_copy.wait()
    for f in range(3):
        mine(f).wait()
    mine_lik.wait()

    @pl.when(rim_here)
    def _():
        pltpu.make_async_copy(out_rim.at[m], state_out.at[rim_slot], own_sem.at[3]).wait()


def finish_kernel(
    slabs, state_in, bed_in, lik_in, water_out, east_out, south_out, weight_out,
    a, b, bed, lik, done, weight, in_sem, out_sem,
):
    m = lax.axis_index("member")
    s = lax.axis_index("space")
    first = s * ROWS
    last_row = slabs * ROWS - 1
    half = ROWS // 2
    cut = 3 * (half + 2 * RIM)
    loads = [
        pltpu.make_async_copy(bed_in, bed, in_sem.at[0]),
        pltpu.make_async_copy(state_in.at[pl.ds(0, cut)], a.at[pl.ds(0, cut)], in_sem.at[1]),
        pltpu.make_async_copy(state_in.at[pl.ds(cut, 3 * EXT - cut)], a.at[pl.ds(cut, 3 * EXT - cut)], in_sem.at[2]),
        pltpu.make_async_copy(lik_in, lik, in_sem.at[3]),
    ]
    for copy in loads[3:] + loads[:3]:
        copy.start()

    def store(row, p, field, value):
        start = p * ROWS * SUB + (row // 8) * (8 * SUB) + lax.rem(row, 8)
        done[field, pl.ds(start, SUB, stride=8)] = value

    copies = []

    def write(part):
        for p in range(PARTS):
            at = pl.ds((2 * p + part) * half * SUB, half * SUB)
            for i, ref in enumerate((east_out, water_out, south_out)):
                copy = pltpu.make_async_copy(done.at[i, at], ref.at[at], out_sem.at[part, p, i])
                copy.start()
                copies.append(copy)

    loads[3].wait()

    members = lik.shape[0] // 2
    rows = lik[0:members] + lik[members : 2 * members]
    own = lax.broadcasted_iota(jnp.int32, rows.shape, 0) == m
    lane = lax.broadcasted_iota(jnp.int32, rows.shape, 2)
    totals = []
    for p in range(PARTS):
        total = jnp.sum(jnp.where(lax.rem(lane, PARTS) == p, rows, 0.0), axis=2, keepdims=True)
        totals.append(-0.5 * jnp.broadcast_to(total, rows.shape))
    top = jnp.max(functools.reduce(jnp.maximum, totals))
    once = lane == 0
    mass = jnp.sum(jnp.where(once, sum(jnp.exp(total - top) for total in totals), 0.0))
    log_mass = jnp.log(jnp.broadcast_to(mass, rows.shape))
    for p in range(PARTS):
        weights = totals[p] - top - log_mass
        weight[p] = jnp.sum(jnp.where(jnp.logical_and(own, once), weights, 0.0))
    copies.append(pltpu.make_async_copy(weight, weight_out, in_sem.at[4]))
    copies[0].start()
    loads[0].wait()
    loads[1].wait()
    step_rows(a, bed, -1, half + 2, 5, first, last_row, keep_in(b, RIM))
    step_rows(b, bed, 0, half, 4, first, last_row, store)
    write(0)
    loads[2].wait()
    step_rows(a, bed, half + 1, half, 4, first, last_row, keep_in(b, RIM))
    step_rows(b, bed, half, half, 4, first, last_row, store)
    write(1)
    for copy in copies:
        copy.wait()


def to_blocks(x):
    lead = x.shape[:-2]
    n = len(lead)
    x = x.reshape(*lead, x.shape[-2] // 8, 8, SUB, LANES)
    x = x.transpose(*range(n), n, n + 2, n + 1, n + 3)
    return x.reshape(-1, LANES)


def from_blocks(x, parts, rows, width):
    x = x.reshape(parts, rows // 8, SUB, 8, LANES).transpose(0, 1, 3, 2, 4)
    return x.reshape(parts, rows, width)


def shards(members, slabs, depth, flow_x, flow_y, terrain, roughness, gauges, observed, ancestors):
    parts, rows, width = depth.shape
    f32 = jnp.float32
    hbm = pl.BlockSpec(memory_space=pl.ANY)
    row = (PARTS, SUB, LANES)
    dma = pltpu.SemaphoreType.DMA
    steps = slabs.bit_length() - 1
    count = gauges.shape[0]
    cells = parts * rows * SUB
    state, bed, lik = pl.pallas_call(
        functools.partial(exchange_kernel, members, slabs),
        out_shape=(
            jax.ShapeDtypeStruct((3 * EXT, *row), f32),
            jax.ShapeDtypeStruct((EXT, 2, SUB, LANES), f32),
            jax.ShapeDtypeStruct((2 * members, 1, LANES), f32),
        ),
        in_specs=[hbm] * 8,
        out_specs=(hbm, hbm, hbm),
        scratch_shapes=[
            pltpu.VMEM((3, cells, LANES), f32),
            pltpu.VMEM((2, rows * SUB, LANES), f32),
            pltpu.VMEM((3 * EXT, *row), f32),
            pltpu.VMEM((3 * EXT, *row), f32),
            pltpu.VMEM((3 * ROWS, *row), f32),
            pltpu.VMEM((EXT, 2, SUB, LANES), f32),
            pltpu.VMEM((members, *row), f32),
            pltpu.VMEM((members, *row), f32),
            pltpu.VMEM((members, *row), f32),
            pltpu.VMEM((members, *row), f32),
            pltpu.VMEM((members, 3, *row), f32),
            pltpu.VMEM((members, *row), f32),
            pltpu.VMEM((rows * SUB, count), jnp.bfloat16),
            pltpu.VMEM((slabs // 2, 1, LANES), f32),
            pltpu.VMEM((1, LANES), f32),
            pltpu.VMEM((1, count), jnp.int32),
            pltpu.VMEM((1, count), f32),
            pltpu.SMEM((members * PARTS,), jnp.int32),
            dma((8,)),
            dma((5,)), dma((5,)),
            dma((3,)), dma((3,)),
            dma((2,)), dma((1,)),
            dma((3,)), dma((3,)),
            dma((1,)), dma((HOLDERS,)),
            dma((1,)), dma((1,)),
            dma((1,)), dma((1,)),
            dma((7,)),
            pltpu.SemaphoreType.REGULAR((2 * steps,)),
        ],
        compiler_params=pltpu.CompilerParams(
            collective_id=0, has_side_effects=True, vmem_limit_bytes=VMEM_LIMIT
        ),
        name="exchange",
    )(
        to_blocks(depth), to_blocks(flow_x), to_blocks(flow_y), to_blocks(terrain), to_blocks(roughness),
        gauges.reshape(1, -1), observed.reshape(1, -1), ancestors,
    )
    water, east, south, weight = pl.pallas_call(
        functools.partial(finish_kernel, slabs),
        out_shape=(jax.ShapeDtypeStruct((cells, LANES), f32),) * 3
        + (jax.ShapeDtypeStruct((parts,), f32),),
        in_specs=[hbm] * 3,
        out_specs=(hbm, hbm, hbm, hbm),
        scratch_shapes=[
            pltpu.VMEM((3 * EXT, *row), f32),
            pltpu.VMEM((3 * EXT, *row), f32),
            pltpu.VMEM((EXT, 2, SUB, LANES), f32),
            pltpu.VMEM((2 * members, 1, LANES), f32),
            pltpu.VMEM((3, cells, LANES), f32),
            pltpu.SMEM((parts,), f32),
            dma((5,)), dma((2, PARTS, 3)),
        ],
        compiler_params=pltpu.CompilerParams(vmem_limit_bytes=VMEM_LIMIT),
        name="finish",
    )(state, bed, lik)
    back = functools.partial(from_blocks, parts=parts, rows=rows, width=width)
    return back(water), back(east), back(south), weight


def solution(mesh):
    placed = (P("member", "space", None),) * 3 + (P("space", None),) * 2 + (P(),) * 3
    return jax.shard_map(
        functools.partial(shards, mesh.shape["member"], mesh.shape["space"]),
        mesh=mesh,
        in_specs=placed,
        out_specs=(P("member", "space", None),) * 3 + (P("member"),),
        check_vma=False,
    )
```
